32 devices in a mesh: sec: 4 (over y, x), bulk: 8 (over z, core).
Axes of the slice: x: 2, y: 2, z: 4, core: 2. Of those that a mesh axis runs over, the one named last changes fastest.
Arguments:
- displacement: float32 [3, 4096], P(None, ('sec', 'bulk')), may hold values from -6 to 6
- nodal_load: float32 [3, 4096], P(None, ('sec', 'bulk')), may hold values from -12 to 12
- connectivity: int32 [4, 16384], P(None, ('sec', 'bulk')), may hold values from 0 to 127
- shape_grads: float32 [12, 16384], P(None, ('sec', 'bulk'))
- elem_volume: float32 [16384], P(('sec', 'bulk')), may hold values from 0.3 to 3
- point_map: int32 [16384], P(('sec', 'bulk')), may hold values from 0 to 16383, as said below
- vol_blocks: int32 [8, 8], P('bulk'), may hold values from 1 to 4, as said below
- c_affine: float32 [8, 8, 36], P('bulk')
- coupling: float32 [20, 8, 6, 128], P(None, 'bulk'), may hold values from -15 to 15
- diag_blocks: bfloat16 [20, 8, 128, 128], P(None, 'bulk'), as said below
- diag_normal: float32 [20, 8, 6], P(None, 'bulk'), may hold values from -4 to 4
- off_blocks: bfloat16 [32, 8, 128, 128], P(None, 'bulk'), may hold values from -0.5 to 0.5
- off_row: int32 [32, 8], P(None, 'bulk'), may hold values from 0 to 19, as said below
- off_col: int32 [32, 8], P(None, 'bulk'), may hold values from 0 to 19, as said below
- off_normal: float32 [32, 8, 6], P(None, 'bulk'), may hold values from -4 to 4
- off_count: int32 [8], P('bulk'), may hold values from 4 to 32, as said below
- fluct_state: bfloat16 [16384, 3072], P(('sec', 'bulk')), as said below
Outputs:
- residual: float32 [3, 4096], P(None, ('sec', 'bulk'))
- product: float32 [3, 4096], P(None, ('sec', 'bulk'))
- update: float32 [3, 4096], P(None, ('sec', 'bulk'))
- fluct_new: bfloat16 [16384, 3072], P(('sec', 'bulk'))
The draws below stay inside these ranges and needn't reach their ends.
Inputs may be any that keep to these rules, and one draw needn't show every extreme that they name: o = point_map[e] // 512 is the serving device, in the order of sec and bulk with sec slowest, and p = point_map[e] % 512 its slot; values are distinct. Device s sends exactly 16 points to every server, 4 of them in volumes with c block rows for each c = 1 .. 4: among the server's slots whose volume has c block rows, taken in increasing order, the one numbered s. `vol_blocks`: each group has 2 volumes of each size from 1 to 4, so 20 block rows in all. `off_row`: A contact's row and column lie in the block rows of one volume of its group, and differ unless that volume has one block row. `off_col`: see off_row. Slots below off_count of a group are in use, the others are not; a multiple of 4, and one group uses all slots. `diag_blocks`: the diagonal entries of every diagonal block lie between 2.5 and 6.5. `fluct_state`: levels a >= the block rows of the point's volume are zero.
All inputs are finite; a program needn't handle non-finite values.
Results may differ from the reference program's by a relative error of at most 0.001.
The reference program's roundings to bfloat16 on the way count: a program that leaves them out, or rounds other values in their place, can miss the bound.
Values may be sent and summed in bfloat16 or wider, within the bound.
No kernel may reach another device: no remote copies, remote signals or barrier semaphores. Data moves between devices by JAX's collectives and lax.ppermute only.
A program may use at most 128 MiB of HBM per device.

```python
import math
import jax
import jax.numpy as jnp
from jax import lax

BS = 128
NBMAX = 4
VOL_GRP = 8
GPV_DEV = 64
SWEEPS = 3
ELEM_DEV = 512
NODE_DEV = 128
ELEMS = 16384
NODES = 4096
CAP = 16
ROWS_GRP = 20
OFF_GRP = 32
N_SEC = 4
N_BULK = 8


def volume_sizes(key):
    key_list = jax.random.split(jax.random.fold_in(key, 101), N_BULK)
    size_cycle = (jnp.arange(VOL_GRP, dtype=jnp.int32) % NBMAX + 1).astype(jnp.int32)
    return jax.vmap(lambda subkey: jax.random.permutation(subkey, size_cycle))(key_list).astype(jnp.int32)


def contact_pattern(key):
    vol_sizes = volume_sizes(key)
    starts = (jnp.cumsum(vol_sizes, axis=1) - vol_sizes).astype(jnp.int32)
    key_list = jax.random.split(jax.random.fold_in(key, 202), 5)
    vol_pick = jax.random.randint(key_list[0], (N_BULK, OFF_GRP), 0, VOL_GRP)
    row_counts = jnp.take_along_axis(vol_sizes, vol_pick, axis=1)
    row_starts = jnp.take_along_axis(starts, vol_pick, axis=1)
    level_one = jax.random.randint(key_list[1], (N_BULK, OFF_GRP), 0, row_counts)
    offset_pick = jax.random.randint(key_list[2], (N_BULK, OFF_GRP), 0, jnp.maximum(row_counts - 1, 1))
    level_two = (level_one + 1 + offset_pick) % row_counts
    load_level = jax.random.randint(key_list[3], (N_BULK,), 1, 5)
    heavy_group = jax.random.randint(key_list[4], (), 0, N_BULK)
    group_ids = jnp.arange(N_BULK, dtype=jnp.int32)
    load_level = jnp.where(group_ids == heavy_group, 8, load_level)
    load_level = jnp.where(group_ids == (heavy_group + 1) % N_BULK, 1, load_level)
    row_pick = (row_starts + level_one).astype(jnp.int32).T
    col_pick = (row_starts + level_two).astype(jnp.int32).T
    return (row_pick, col_pick, (load_level * (OFF_GRP // 8)).astype(jnp.int32))


def draw_point_map(key, part):
    devices = N_SEC * N_BULK
    per_class = CAP // NBMAX
    vol_sizes = volume_sizes(key)
    vol_ids = jnp.arange(VOL_GRP, dtype=jnp.int32)
    earlier = (vol_sizes[:, None, :] == vol_sizes[:, :, None]) & (vol_ids[None, None, :] < vol_ids[None, :, None])
    vol_rank = jnp.sum(earlier.astype(jnp.int32), axis=2).astype(jnp.int32)
    slot_ids = jnp.arange(ELEM_DEV, dtype=jnp.int32)
    slot_rank = vol_rank[:, slot_ids // GPV_DEV] * GPV_DEV + slot_ids[None, :] % GPV_DEV
    slot_class = vol_sizes[:, slot_ids // GPV_DEV]
    slot_code = (slot_rank // per_class * NBMAX + slot_class - 1) * per_class + slot_rank % per_class
    group_rows = jnp.broadcast_to(jnp.arange(N_BULK, dtype=jnp.int32)[:, None], (N_BULK, ELEM_DEV))
    slot_table = jnp.zeros((N_BULK, ELEM_DEV), jnp.int32).at[group_rows, slot_code].set(jnp.broadcast_to(slot_ids[None, :], (N_BULK, ELEM_DEV)))
    key_list = jax.random.split(jax.random.fold_in(key, 303), devices)
    shuffles = jax.vmap(lambda subkey: jax.random.permutation(subkey, ELEM_DEV))(key_list).astype(jnp.int32)
    source = jnp.arange(devices, dtype=jnp.int32)[:, None]
    owner_id = shuffles // CAP
    position = shuffles % CAP
    chosen_slot = slot_table[owner_id % N_BULK, source * CAP + position]
    return (owner_id * ELEM_DEV + chosen_slot).reshape(-1).astype(jnp.int32)


def draw_vol_blocks(key, part):
    return volume_sizes(key)


def draw_off_row(key, part):
    return contact_pattern(key)[0]


def draw_off_col(key, part):
    return contact_pattern(key)[1]


def draw_off_count(key, part):
    return contact_pattern(key)[2]


def draw_shape_grads(key, part):
    devices = N_SEC * N_BULK
    position = (jnp.arange(ELEMS, dtype=jnp.int32) // ELEM_DEV).astype(jnp.float32) / max(devices - 1, 1)
    subkey = jax.random.fold_in(key, 505)
    entries = 0.3 * jax.random.normal(subkey, (12, ELEMS), jnp.float32)
    growth = 3.0 ** (0.25 * position)
    return entries * growth[None, :]


def draw_c_affine(key, part):
    key_list = jax.random.split(jax.random.fold_in(key, 606), 2)
    gaussian = jax.random.normal(key_list[0], (N_BULK, VOL_GRP, 6, 6), jnp.float32)
    symmetric = 0.25 * (gaussian + jnp.swapaxes(gaussian, 2, 3))
    diag_vals = jax.random.uniform(key_list[1], (N_BULK, VOL_GRP, 6), jnp.float32, 4.0, 6.0)
    identity = jnp.eye(6, dtype=jnp.float32)
    full = symmetric * (1.0 - identity) + identity * diag_vals[:, :, :, None]
    return full.reshape(N_BULK, VOL_GRP, 36)


def draw_diag_blocks(key, part):
    key_list = jax.random.split(jax.random.fold_in(key, 707), 2)
    full_shape = (ROWS_GRP, N_BULK, BS, BS)
    identity = jnp.eye(BS, dtype=bool)
    off_entries = 0.22 * jax.random.normal(key_list[0], full_shape, jnp.float32)
    diag_entries = jax.random.uniform(key_list[1], full_shape, jnp.float32, 3.0, 6.0)
    return jnp.where(identity, diag_entries, off_entries).astype(jnp.bfloat16)


def draw_fluct_state(key, part):
    slot_codes = draw_point_map(key, part)
    vol_sizes = volume_sizes(key)
    owner_id = slot_codes // ELEM_DEV
    within = slot_codes % ELEM_DEV
    row_counts = vol_sizes[owner_id % N_BULK, within // GPV_DEV]
    live_rows = (jnp.arange(NBMAX, dtype=jnp.int32)[None, :] < row_counts[:, None]).astype(jnp.float32)
    subkey = jax.random.fold_in(key, 404)
    entries = 0.5 * jax.random.normal(subkey, (ELEMS, NBMAX, BS * 6), jnp.float32)
    return (entries * live_rows[:, :, None]).reshape(ELEMS, NBMAX * BS * 6).astype(jnp.bfloat16)


def set_ends(values, rng, smallest, largest):
    place = [jax.random.randint(jax.random.fold_in(rng, axis), (), 0, length) for axis, length in enumerate(values.shape)]
    widest = values.shape.index(max(values.shape))
    next_to = place[:widest] + [(place[widest] + 1) % values.shape[widest]] + place[widest + 1:]
    return values.at[tuple(place)].set(smallest).at[tuple(next_to)].set(largest)


def block_levels(rng, shape, shards, low, largest):
    def one(dim, parts):
        steps = jax.random.uniform(jax.random.fold_in(jax.random.fold_in(rng, 6), dim), (parts,), jnp.float32, low / len(shards), largest / len(shards))
        return jnp.repeat(jnp.exp(steps), shape[dim] // parts).reshape((-1,) + (1,) * (len(shape) - dim - 1))

    loudness = one(*shards[0])
    for cut in shards[1:]:
        loudness = loudness * one(*cut)
    return loudness


def normal_values(stream_key, shape, scale, reach, cuts=(), held_as=jnp.bfloat16):
    drawn = scale * jax.random.normal(stream_key, shape, jnp.float32)
    if cuts:
        drawn = drawn * block_levels(stream_key, shape, cuts, -0.22, 0.18)
    return jnp.clip(drawn, -reach, reach).astype(held_as)


def setup_inputs(seed: int = 0) -> dict:
    key_of = jax.random.split(jax.random.key(seed), 18)
    displacement = normal_values(key_of[0], (3, NODES), 1.0, 6.0, ((1, 32),), jnp.float32)
    nodal_load = normal_values(key_of[1], (3, NODES), 2.0, 12.0, ((1, 32),), jnp.float32)
    connectivity = set_ends(jax.random.randint(key_of[2], (4, ELEMS), 0, NODE_DEV), jax.random.fold_in(key_of[2], 1), 0, NODE_DEV - 1).astype(jnp.int32)
    shape_grads = draw_shape_grads(jax.random.fold_in(key_of[17], 71), 0)
    elem_volume = jnp.clip(jnp.exp(math.log(3.0) - 2.3025851 * jax.random.uniform(key_of[4], (ELEMS,), jnp.float32) ** block_levels(key_of[4], (ELEMS,), ((0, 32),), -0.2, 0.2)), 0.3, 3.0)
    point_map = draw_point_map(jax.random.fold_in(key_of[17], 71), 0)
    vol_blocks = draw_vol_blocks(jax.random.fold_in(key_of[17], 71), 0)
    c_affine = draw_c_affine(jax.random.fold_in(key_of[17], 71), 0)
    coupling = normal_values(key_of[8], (ROWS_GRP, N_BULK, 6, BS), 2.5, 15.0, ((1, 8),), jnp.float32)
    diag_blocks = draw_diag_blocks(jax.random.fold_in(key_of[17], 71), 0)
    diag_normal = normal_values(key_of[10], (ROWS_GRP, N_BULK, 6), 0.7, 4.0, ((1, 8),), jnp.float32)
    off_blocks = normal_values(key_of[11], (OFF_GRP, N_BULK, BS, BS), 0.08, 0.5, ((1, 8),))
    off_row = draw_off_row(jax.random.fold_in(key_of[17], 71), 0)
    off_col = draw_off_col(jax.random.fold_in(key_of[17], 71), 0)
    off_normal = normal_values(key_of[14], (OFF_GRP, N_BULK, 6), 0.7, 4.0, ((1, 8),), jnp.float32)
    off_count = draw_off_count(jax.random.fold_in(key_of[17], 71), 0)
    fluct_state = draw_fluct_state(jax.random.fold_in(key_of[17], 71), 0)
    return {"displacement": displacement, "nodal_load": nodal_load, "connectivity": connectivity, "shape_grads": shape_grads, "elem_volume": elem_volume, "point_map": point_map, "vol_blocks": vol_blocks, "c_affine": c_affine, "coupling": coupling, "diag_blocks": diag_blocks, "diag_normal": diag_normal, "off_blocks": off_blocks, "off_row": off_row, "off_col": off_col, "off_normal": off_normal, "off_count": off_count, "fluct_state": fluct_state}


HIGHEST_PREC = lax.Precision.HIGHEST
GAIN_NORMAL = 0.4
CLIP_RMS = 1.0

def strain_of(shape_grads, nodal):
    shaped = shape_grads.reshape(4, 3, -1)
    grad_x, grad_y, grad_z = (shaped[:, 0], shaped[:, 1], shaped[:, 2])
    disp_x, disp_y, disp_z = (nodal[0], nodal[1], nodal[2])
    return jnp.stack([lax.optimization_barrier(jnp.sum(grad_x * disp_x, axis=0)), lax.optimization_barrier(jnp.sum(grad_y * disp_y, axis=0)), lax.optimization_barrier(jnp.sum(grad_z * disp_z, axis=0)), lax.optimization_barrier(jnp.sum(grad_z * disp_y + grad_y * disp_z, axis=0)), lax.optimization_barrier(jnp.sum(grad_z * disp_x + grad_x * disp_z, axis=0)), lax.optimization_barrier(jnp.sum(grad_y * disp_x + grad_x * disp_y, axis=0))])

def forces_of(shape_grads, stress):
    shaped = shape_grads.reshape(4, 3, -1)
    grad_x, grad_y, grad_z = (shaped[:, 0], shaped[:, 1], shaped[:, 2])
    force_x = grad_x * stress[0] + grad_z * stress[4] + grad_y * stress[5]
    force_y = grad_y * stress[1] + grad_z * stress[3] + grad_x * stress[5]
    force_z = grad_z * stress[2] + grad_y * stress[3] + grad_x * stress[4]
    return jnp.stack([force_x, force_y, force_z])

def apply_tangent(tangent_cols, strain):
    return lax.optimization_barrier(jnp.sum(tangent_cols.reshape(6, 6, -1) * strain[None, :, :], axis=1))

def assemble(forces, node_ids, node_total):
    flat_ids = node_ids.reshape(-1)
    return jnp.stack([jax.ops.segment_sum(forces[component].reshape(-1), flat_ids, num_segments=node_total) for component in range(3)])

def row_layout(vol_sizes):
    row_ends = jnp.cumsum(vol_sizes).astype(jnp.int32)
    starts = (row_ends - vol_sizes).astype(jnp.int32)
    row_ids = jnp.arange(ROWS_GRP, dtype=jnp.int32)
    row_volume = lax.optimization_barrier(jnp.sum((row_ids[:, None] >= row_ends[None, :]).astype(jnp.int32), axis=1)).astype(jnp.int32)
    onehot = jnp.arange(VOL_GRP, dtype=jnp.int32)[:, None] == row_volume[None, :]
    row_level = (row_ids - lax.optimization_barrier(jnp.sum(jnp.where(onehot, starts[:, None], 0), axis=0))).astype(jnp.int32)
    return (row_volume, onehot.astype(jnp.float32), (row_volume * NBMAX + row_level).astype(jnp.int32))

def state_rows(state_slots, gather_index):
    shaped = state_slots.reshape(VOL_GRP, GPV_DEV, NBMAX, BS, 6)
    reordered = jnp.transpose(shaped, (0, 2, 3, 1, 4)).reshape(VOL_GRP * NBMAX, BS, GPV_DEV * 6)
    return reordered[gather_index]

def rows_state(row_values, gather_index):
    padded = jnp.zeros((VOL_GRP * NBMAX, BS, GPV_DEV * 6), row_values.dtype).at[gather_index].set(row_values)
    shaped = padded.reshape(VOL_GRP, NBMAX, BS, GPV_DEV, 6)
    return jnp.transpose(shaped, (0, 3, 1, 2, 4)).reshape(VOL_GRP * GPV_DEV, NBMAX * BS * 6)

def micro_solve(strain_slots, state_slots, vol_sizes, c_affine, coupling, diag_blk, diag_nrm, off_blk, off_rows, off_cols, off_nrm, live_count):
    row_volume, onehot, gather_index = row_layout(vol_sizes)
    strain_vg = strain_slots.astype(jnp.float32).reshape(VOL_GRP, GPV_DEV, 6)
    strain_rows = jnp.einsum('vr,vgk->rgk', onehot, strain_vg, precision=HIGHEST_PREC)
    diag_scale = 1.0 + GAIN_NORMAL * jnp.tanh(jnp.einsum('rk,rgk->rg', diag_nrm, strain_rows, precision=HIGHEST_PREC))
    diag_cols = jnp.repeat(diag_scale, 6, axis=1)
    off_strain = strain_vg[row_volume[off_rows]]
    live_mask = (jnp.arange(OFF_GRP, dtype=jnp.int32) < live_count).astype(jnp.float32)
    off_scale = (1.0 + GAIN_NORMAL * jnp.tanh(jnp.einsum('ok,ogk->og', off_nrm, off_strain, precision=HIGHEST_PREC))) * live_mask[:, None]
    off_scale_cols = jnp.repeat(off_scale, 6, axis=1)
    diag_vals = jnp.diagonal(diag_blk, axis1=1, axis2=2).astype(jnp.float32)
    load_rows = jnp.tile(jnp.swapaxes(coupling, 1, 2), (1, 1, GPV_DEV))
    denominator = diag_vals[:, :, None] * diag_cols[:, None, :]
    fluctuation = state_rows(state_slots, gather_index).astype(jnp.float32)
    diag_wide = diag_blk.astype(jnp.float32)
    off_wide = off_blk.astype(jnp.float32)
    for sweep_index in range(SWEEPS):
        fluct_low = fluctuation.astype(jnp.bfloat16)
        fluct_wide = fluct_low.astype(jnp.float32)
        applied = jnp.einsum('rab,rbc->rac', diag_wide, fluct_wide, precision=HIGHEST_PREC) * diag_cols[:, None, :]
        contact = jnp.einsum('oab,obc->oac', off_wide, fluct_wide[off_cols], precision=HIGHEST_PREC) * off_scale_cols[:, None, :]
        applied = applied.at[off_rows].add(contact)
        fluctuation = fluctuation + (load_rows - applied) / denominator
    projection = jnp.einsum('rid,rdc->ric', coupling, fluctuation, precision=HIGHEST_PREC)
    vol_proj = jnp.einsum('vr,ric->vic', onehot, projection, precision=HIGHEST_PREC)
    vol_proj = vol_proj / (vol_sizes.astype(jnp.float32) * BS)[:, None, None]
    tangent = c_affine.reshape(VOL_GRP, 6, 1, 6) - vol_proj.reshape(VOL_GRP, 6, GPV_DEV, 6)
    tangent = jnp.transpose(tangent, (0, 2, 1, 3)).reshape(VOL_GRP * GPV_DEV, 36).astype(jnp.bfloat16)
    state_new = rows_state(fluctuation.astype(jnp.bfloat16), gather_index)
    return (tangent, state_new)

def reference(displacement, nodal_load, connectivity, shape_grads, elem_volume, point_map, vol_blocks, c_affine, coupling, diag_blocks, diag_normal, off_blocks, off_row, off_col, off_normal, off_count, fluct_state):
    devices = N_SEC * N_BULK
    element_ids = jnp.arange(ELEMS, dtype=jnp.int32)
    node_ids = (connectivity + (element_ids // ELEM_DEV)[None, :] * NODE_DEV).astype(jnp.int32)
    strain = strain_of(shape_grads, displacement[:, node_ids])
    strain_sent = strain.T.astype(jnp.bfloat16)
    arrival_from = jnp.zeros((ELEMS,), jnp.int32).at[point_map].set(element_ids)

    def serve(state_pair, owner_id):
        tangent_all, fluct_all = state_pair
        group_id = owner_id % N_BULK
        members = lax.dynamic_slice_in_dim(arrival_from, owner_id * ELEM_DEV, ELEM_DEV)
        tangent, state_new = micro_solve(strain_sent[members], fluct_state[members], vol_blocks[group_id], c_affine[group_id], coupling[:, group_id], diag_blocks[:, group_id], diag_normal[:, group_id], off_blocks[:, group_id], off_row[:, group_id], off_col[:, group_id], off_normal[:, group_id], off_count[group_id])
        return ((tangent_all.at[members].set(tangent), fluct_all.at[members].set(state_new)), None)
    initial = (jnp.zeros((ELEMS, 36), jnp.bfloat16), jnp.zeros((ELEMS, NBMAX * BS * 6), jnp.bfloat16))
    scanned, unused = lax.scan(serve, initial, jnp.arange(devices, dtype=jnp.int32))
    tangent_all, fluct_new = scanned
    tangent_cols = tangent_all.astype(jnp.float32).T
    weights = elem_volume[None, :]
    stress = apply_tangent(tangent_cols, strain)
    residual = assemble(forces_of(shape_grads, weights * stress), node_ids, NODES) - nodal_load
    norm_sq = jnp.sum(residual * residual)
    root_mean = jnp.sqrt(norm_sq / (3.0 * NODES) + 1e-06)
    update = -jnp.minimum(1.0, CLIP_RMS / root_mean) * residual
    trial_strain = strain_of(shape_grads, residual[:, node_ids])
    product = assemble(forces_of(shape_grads, weights * apply_tangent(tangent_cols, trial_strain)), node_ids, NODES)
    return (residual, product, update, fluct_new)
```

```python
import functools

import jax
import jax.numpy as jnp
from jax import lax
from jax.experimental import pallas as pl
from jax.experimental.pallas import tpu as pltpu
from jax.sharding import Mesh, PartitionSpec as P

BS = 128
NBMAX = 4
VOL_GRP = 8
GPV_DEV = 64
SWEEPS = 3
ROWS_GRP = 20
HALF_ROWS = 10
OFF_GRP = 32
HALF_OFF = 16
COMPS = 6
LEVEL = BS * COMPS
UNIT = 8
TILE = 16
SLOTS = UNIT * TILE
STATE_LANES = 5 * LEVEL
MSG_LANES = STATE_LANES + 128
GAIN_NORMAL = 0.4
CLIP_RMS = 1.0
SM_DIAG_NORMAL = 80
SM_OFF_NORMAL = 96
SM_AFFINE = 128
SM_ROWS = 136

F32 = jnp.float32
BF16 = jnp.bfloat16
I32 = jnp.int32
AXES = ("y", "x", "h", "l", "c")
GROUP_AXES = ("h", "l", "c")
UNIT_AXES = ("x", "l", "c")
VMEM_LIMIT = 56 * 1024 * 1024

CLASS_PLACE = ((4 * LEVEL, 0), (3 * LEVEL, TILE), (0, TILE), (0, 0))
CLASS_BASE = (0, 1, 3, 6)


def dot_nn(lhs, rhs):
    return lax.dot_general(lhs, rhs, (((1,), (0,)), ((), ())), preferred_element_type=F32)


def dot_nt(lhs, rhs):
    return lax.dot_general(lhs, rhs, (((1,), (1,)), ((), ())), preferred_element_type=F32)


def dot_tn(lhs, rhs):
    return lax.dot_general(lhs, rhs, (((0,), (0,)), ((), ())), preferred_element_type=F32)


def split3(value):
    high = value.astype(BF16)
    rest = value - high.astype(F32)
    mid = rest.astype(BF16)
    low = (rest - mid.astype(F32)).astype(BF16)
    return high, mid, low


def iota(shape, dim):
    return lax.broadcasted_iota(I32, shape, dim)


def lane_order():
    target = iota((1, LEVEL), 1)
    source = COMPS * (target % BS) + target // BS
    return jnp.where(iota((LEVEL, LEVEL), 0) == source, 1.0, 0.0).astype(BF16)


def class_onehot(slot, size, level_rows):
    chosen = jnp.where(size == level_rows, slot, -1)
    return jnp.where(iota((SLOTS, slot.shape[1]), 0) == chosen, 1.0, 0.0).astype(BF16)


def node_onehot(conn_row, nodes):
    return jnp.where(iota((nodes, conn_row.shape[1]), 0) == conn_row, 1.0, 0.0).astype(BF16)


def nodal_parts(nodal):
    parts = [jnp.concatenate([p.astype(F32), jnp.zeros((13, p.shape[1]), F32)], axis=0) for p in split3(nodal)]
    rows = parts[0] + pltpu.roll(parts[1], 3, 0) + pltpu.roll(parts[2], 6, 0)
    return rows.astype(BF16)


def gather_nodes(rows, onehots):
    found = []
    for onehot in onehots:
        got = dot_nn(rows, onehot)
        found.append([got[i : i + 1] + got[i + 3 : i + 4] + got[i + 6 : i + 7] for i in range(3)])
    return found


def strain_rows(grads, disp):
    g = lambda a, k: grads[3 * a + k : 3 * a + k + 1]
    total = lambda f: f(0) + f(1) + f(2) + f(3)
    return [
        total(lambda a: g(a, 0) * disp[a][0]),
        total(lambda a: g(a, 1) * disp[a][1]),
        total(lambda a: g(a, 2) * disp[a][2]),
        total(lambda a: g(a, 2) * disp[a][1] + g(a, 1) * disp[a][2]),
        total(lambda a: g(a, 2) * disp[a][0] + g(a, 0) * disp[a][2]),
        total(lambda a: g(a, 1) * disp[a][0] + g(a, 0) * disp[a][1]),
    ]


def matrix_pack_kernel(
    ids, vol, off_row, off_col, off_count, coupling, diag_normal, off_normal, affine, diag, off,
    blocks, small, ints, row_local, row_size, rows_sel, seen, sems,
):
    half = ids[0]
    small[...] = jnp.zeros_like(small)
    for size in range(NBMAX + 1):
        seen[size] = 0
    start = 0
    for v in range(VOL_GRP):
        size = vol[0, v]
        rank = seen[size]
        seen[size] = rank + 1
        mine = rank == half
        base = (size * (size - 1)) // 2
        for a in range(NBMAX):
            @pl.when(a < size)
            def _(a=a, size=size, base=base, mine=mine, start=start):
                row_local[start + a] = jnp.where(mine, base + a, -1)
                row_size[start + a] = size - 1

            @pl.when(jnp.logical_and(a < size, mine))
            def _(a=a, base=base, start=start):
                rows_sel[base + a] = start + a

        @pl.when(mine)
        def _(size=size, v=v):
            small[pl.ds(SM_AFFINE - 1 + size, 1), 0:36] = affine[v : v + 1, :]

        start = start + size
    copies = [
        pltpu.make_async_copy(
            off.at[pl.ds(half * HALF_OFF, HALF_OFF)], blocks.at[pl.ds(HALF_ROWS, HALF_OFF)], sems.at[HALF_ROWS]
        )
    ]
    for i in range(HALF_ROWS):
        copies.append(
            pltpu.make_async_copy(diag.at[pl.ds(rows_sel[i], 1)], blocks.at[pl.ds(i, 1)], sems.at[i])
        )
    for copy in copies:
        copy.start()
    for i in range(HALF_ROWS):
        row = rows_sel[i]
        small[8 * i : 8 * i + COMPS, :] = coupling[row]
        small[SM_DIAG_NORMAL + i : SM_DIAG_NORMAL + i + 1, 0:COMPS] = diag_normal[pl.ds(row, 1), :]

    @pl.when(half == 0)
    def _():
        small[SM_OFF_NORMAL : SM_OFF_NORMAL + OFF_GRP, 0:COMPS] = off_normal[...]

    @pl.when(half != 0)
    def _():
        small[SM_OFF_NORMAL : SM_OFF_NORMAL + HALF_OFF, 0:COMPS] = off_normal[HALF_OFF:, :]
        small[SM_OFF_NORMAL + HALF_OFF : SM_OFF_NORMAL + OFF_GRP, 0:COMPS] = off_normal[:HALF_OFF, :]

    live_total = off_count[0]

    def contact(n, found):
        slot = (n + half * HALF_OFF) % OFF_GRP
        row = off_row[slot, 0]
        local = row_local[row]
        ints[5, n] = row_size[row]
        live = jnp.logical_and(slot < live_total, local >= 0)

        @pl.when(live)
        def _():
            ints[1, found] = n
            ints[2, found] = local
            ints[3, found] = row_local[off_col[slot, 0]]

        return found + live.astype(I32)

    ints[0, 0] = lax.fori_loop(0, OFF_GRP, contact, 0)
    for copy in copies:
        copy.wait()


def pack_kernel(groups, rounds, ids, point_map, table, disp, conn, grads, state, *refs):
    outs, (strain_out, place_out, state_vmem, sem) = refs[:UNIT], refs[UNIT:]
    load = pltpu.make_async_copy(state, state_vmem, sem)
    load.start()
    elems = point_map.shape[1]
    x_me, h_me, l_me, c_me = ids[1], ids[2], ids[3], ids[4]
    z_count = groups // 4
    codes = point_map[...]
    owner = codes // elems
    within = codes % elems
    group = owner % groups
    volume = within // GPV_DEV
    delta = (group // 4 - h_me + z_count) % z_count
    core = group % 2
    low = (group // 2) % 2
    across = (delta % 2) ^ core
    turn = delta // 2
    offset = ((across ^ x_me) * 4) + ((low ^ l_me) * 2) + (core ^ c_me)
    group_hot = jnp.where(iota((groups, elems), 0) == group, 1.0, 0.0).astype(BF16)
    sizes = dot_tn(table[...].astype(F32).astype(BF16), group_hot)
    size = jnp.sum(
        jnp.where(iota((VOL_GRP, elems), 0) == volume, sizes, 0.0), axis=0, keepdims=True
    ).astype(I32)
    key = (offset * NBMAX + size - 1) * rounds + turn
    key_hot = iota((UNIT * NBMAX * rounds, elems), 0) == key
    earlier = jnp.where(iota((elems, elems), 0) < iota((elems, elems), 1), 1.0, 0.0).astype(BF16)
    counts = dot_nn(jnp.where(key_hot, 1.0, 0.0).astype(BF16), earlier)
    rank = jnp.sum(jnp.where(key_hot, counts, 0.0), axis=0, keepdims=True).astype(I32)
    slot = offset * TILE + turn * (TILE // rounds) + rank
    place_out[...] = jnp.concatenate([slot, size, jnp.zeros((6, elems), I32)], axis=0)

    nodes = disp.shape[1]
    onehots = [node_onehot(conn[a : a + 1, :], nodes) for a in range(4)]
    found = gather_nodes(nodal_parts(disp[...]), onehots)
    strain = strain_rows(grads[...], found)
    strain8 = jnp.concatenate(strain + [jnp.zeros((2, elems), F32)], axis=0)
    strain_out[...] = strain8
    first = jnp.concatenate([strain8, jnp.zeros((120, elems), F32)], axis=0).astype(BF16)
    second = jnp.concatenate(
        [jnp.zeros((64, elems), F32), strain8, jnp.zeros((56, elems), F32)], axis=0
    ).astype(BF16)
    hots = [class_onehot(slot, size, c + 1) for c in range(NBMAX)]
    for one, other, row0 in ((3, 0, 0), (2, 1, TILE)):
        extras = (dot_nt(hots[one], first) + dot_nt(hots[other], second)).astype(BF16)
        for k in range(UNIT):
            outs[k][row0 : row0 + TILE, STATE_LANES:] = extras[TILE * k : TILE * (k + 1)]
    order = lane_order()
    load.wait()
    for c in range(NBMAX):
        lane0, row0 = CLASS_PLACE[c]
        for a in range(c + 1):
            rows = dot_nn(hots[c], state_vmem[:, LEVEL * a : LEVEL * (a + 1)]).astype(BF16)
            rows = dot_nn(rows, order).astype(BF16)
            for k in range(UNIT):
                outs[k][row0 : row0 + TILE, lane0 + LEVEL * a : lane0 + LEVEL * (a + 1)] = rows[
                    TILE * k : TILE * (k + 1)
                ]


def solve_kernel(ids, ints, small, blocks, other, *refs):
    msgs, refs = refs[:UNIT], refs[UNIT:]
    outs, refs = refs[:UNIT], refs[UNIT:]
    tangents, state, low, acc, contact_scale, diag_scale, inverse, response, diag_pairs, off_pairs = refs
    for c in range(NBMAX):
        lane0, row0 = CLASS_PLACE[c]
        for a in range(c + 1):
            r = CLASS_BASE[c] + a
            for j in range(COMPS):
                lane = lane0 + LEVEL * a + BS * j
                for k in range(UNIT):
                    piece = msgs[k][row0 : row0 + TILE, lane : lane + BS]
                    dst = slice(SLOTS * j + TILE * k, SLOTS * j + TILE * (k + 1))
                    low[r, dst, :] = piece
                    state[r, dst, :] = piece.astype(F32)
    normals = small[SM_DIAG_NORMAL : SM_OFF_NORMAL + OFF_GRP, :]
    shifted = pltpu.roll(normals, 64, 1)
    for rows, one, two in ((0, 3, 0), (TILE, 2, 1)):
        strains = jnp.concatenate([msgs[k][rows : rows + TILE, STATE_LANES:] for k in range(UNIT)], axis=0)
        for cls, vectors in ((one, normals), (two, shifted)):
            high, mid, lowest = split3(vectors)
            dots = dot_nt(strains, high) + dot_nt(strains, mid) + dot_nt(strains, lowest)
            response[cls, :, 0 : dots.shape[1]] = 1.0 + GAIN_NORMAL * jnp.tanh(dots)
    eye = iota((BS, BS), 0) == iota((BS, BS), 1)
    for c in range(NBMAX):
        for a in range(c + 1):
            r = CLASS_BASE[c] + a
            scale = jnp.broadcast_to(response[c, :, r : r + 1], (SLOTS, BS))
            diag_scale[r] = scale
            values = jnp.sum(jnp.where(eye, blocks[r].astype(F32), 0.0), axis=0, keepdims=True)
            inverse[r] = 1.0 / (scale * values)
    for n in range(OFF_GRP):
        contact_scale[n] = jnp.broadcast_to(
            response[ints[5, n], :, HALF_OFF + n : HALF_OFF + n + 1], (SLOTS, BS)
        )
    zero = jnp.zeros((BS, BS), BF16)
    for p in range(HALF_ROWS // 2):
        diag_pairs[p, :BS, :BS] = blocks[2 * p]
        diag_pairs[p, :BS, BS:] = zero
        diag_pairs[p, BS:, :BS] = zero
        diag_pairs[p, BS:, BS:] = blocks[2 * p + 1]
    live = ints[0, 0]
    pairs = (live + 1) // 2

    def contact_block(n):
        mine = n < HALF_OFF
        own = blocks[HALF_ROWS + jnp.where(mine, n, 0)]
        theirs = other[jnp.where(mine, 0, n - HALF_OFF)]
        return jnp.where(mine, own, theirs)

    def fill(p, carry):
        off_pairs[p, :BS, :BS] = contact_block(ints[1, 2 * p])
        off_pairs[p, :BS, BS:] = zero
        off_pairs[p, BS:, :BS] = zero
        has_second = 2 * p + 1 < live

        @pl.when(has_second)
        def _():
            off_pairs[p, BS:, BS:] = contact_block(ints[1, 2 * p + 1])

        @pl.when(jnp.logical_not(has_second))
        def _():
            off_pairs[p, BS:, BS:] = zero

        return carry

    lax.fori_loop(0, pairs, fill, 0)

    def sweep(step, carry):
        for p in range(HALF_ROWS // 2):
            both = jnp.concatenate([low[2 * p], low[2 * p + 1]], axis=1)
            product = dot_nt(both, diag_pairs[p])
            for i in range(2):
                r = 2 * p + i
                scale = diag_scale[r]
                for j in range(COMPS):
                    rows = slice(SLOTS * j, SLOTS * (j + 1))
                    acc[r, rows, :] = product[rows, BS * i : BS * (i + 1)] * scale

        def contact(p, inner):
            second = jnp.minimum(2 * p + 1, live - 1)
            slots = (2 * p, second)
            both = jnp.concatenate([low[ints[3, m]] for m in slots], axis=1)
            product = dot_nt(both, off_pairs[p])
            for i, m in enumerate(slots):
                r = ints[2, m]
                scale = contact_scale[ints[1, m]]
                for j in range(COMPS):
                    rows = slice(SLOTS * j, SLOTS * (j + 1))
                    acc[r, rows, :] += product[rows, BS * i : BS * (i + 1)] * scale
            return inner

        lax.fori_loop(0, pairs, contact, 0)
        for r in range(HALF_ROWS):
            inv = inverse[r]
            for j in range(COMPS):
                rows = slice(SLOTS * j, SLOTS * (j + 1))
                load = small[8 * r + j : 8 * r + j + 1, :]
                value = state[r, rows, :] + (load - acc[r, rows, :]) * inv
                state[r, rows, :] = value
                low[r, rows, :] = value.astype(BF16)
        return carry

    lax.fori_loop(0, SWEEPS, sweep, 0)
    lane = iota((1, BS), 1)
    comp = lane // 8
    for c in range(NBMAX):
        total = jnp.zeros((SLOTS, BS), F32)
        for a in range(c + 1):
            r = CLASS_BASE[c] + a
            load8 = small[8 * r : 8 * r + 8, :]
            tiled = jnp.concatenate([load8] * 6 + [jnp.zeros((80, BS), F32)], axis=0)
            weights = jnp.concatenate(split3(tiled)[:2], axis=0)
            value = state[r]
            high = value.astype(BF16)
            rest = (value - high.astype(F32)).astype(BF16)
            product = dot_nt(high, weights) + dot_nt(rest, weights)
            product = product[:, :BS] + product[:, BS:]
            for j in range(COMPS):
                total += jnp.where(comp == j, product[SLOTS * j : SLOTS * (j + 1)], 0.0)
        source = iota((BS, BS), 0)
        target = iota((BS, BS), 1)
        wanted = jnp.logical_and(
            source == 6 * (target % 8) + target // 8, jnp.logical_and(target % 8 < 6, target < 48)
        )
        moved = jnp.sum(
            jnp.where(wanted, jnp.transpose(jnp.broadcast_to(small[SM_AFFINE + c : SM_AFFINE + c + 1, :], (BS, BS))), 0.0),
            axis=0,
            keepdims=True,
        )
        acc[c, :SLOTS, :] = moved - total / ((c + 1) * BS)
    for row0, one, two in ((0, 3, 0), (TILE, 2, 1)):
        first = acc[one, :SLOTS, :]
        second = acc[two, :SLOTS, :]
        packed = jnp.where(lane < 64, first, pltpu.roll(second, 64, 1)).astype(BF16)
        for k in range(UNIT):
            tangents[ids[5] ^ k, row0 : row0 + TILE, :] = packed[TILE * k : TILE * (k + 1)]
    for c in range(NBMAX):
        lane0, row0 = CLASS_PLACE[c]
        for a in range(c + 1):
            r = CLASS_BASE[c] + a
            for j in range(COMPS):
                lane_at = lane0 + LEVEL * a + BS * j
                for k in range(UNIT):
                    outs[k][row0 : row0 + TILE, lane_at : lane_at + BS] = low[
                        r, SLOTS * j + TILE * k : SLOTS * j + TILE * (k + 1), :
                    ]


def fem_kernel(ids, tangents, place, strain, grads, volume, conn, nodal_load, residual, product, norm):
    elems = place.shape[1]
    nodes = nodal_load.shape[1]
    slot, size = place[0:1, :], place[1:2, :]
    hots = [class_onehot(slot, size, c + 1) for c in range(NBMAX)]
    entries = jnp.zeros((64, elems), F32)
    for row0, one, two in ((0, 3, 0), (TILE, 2, 1)):
        packed = jnp.concatenate([tangents[ids[5] ^ k, row0 : row0 + TILE, :] for k in range(UNIT)], axis=0)
        entries += dot_tn(packed, hots[one])[:64]
        entries += dot_tn(packed, hots[two])[64:]
    entry = lambda i, j: entries[8 * j + i : 8 * j + i + 1]
    weight = volume[...]
    g_all = grads[...]
    g = lambda a, k: g_all[3 * a + k : 3 * a + k + 1]
    onehots = [node_onehot(conn[a : a + 1, :], nodes) for a in range(4)]

    def assemble(strains):
        s = []
        for i in range(COMPS):
            total = entry(i, 0) * strains[0]
            for j in range(1, COMPS):
                total = total + entry(i, j) * strains[j]
            s.append(total * weight)
        result = jnp.zeros((TILE, nodes), F32)
        for a in range(4):
            force = jnp.concatenate(
                [
                    g(a, 0) * s[0] + g(a, 2) * s[4] + g(a, 1) * s[5],
                    g(a, 1) * s[1] + g(a, 2) * s[3] + g(a, 0) * s[5],
                    g(a, 2) * s[2] + g(a, 1) * s[3] + g(a, 0) * s[4],
                ],
                axis=0,
            )
            result += dot_nt(nodal_parts(force), onehots[a])
        return result[0:3] + result[3:6] + result[6:9]

    strains = strain[...]
    res = assemble([strains[i : i + 1] for i in range(COMPS)]) - nodal_load[...]
    residual[...] = res
    norm[...] = jnp.broadcast_to(jnp.sum(res * res, keepdims=True), norm.shape)
    trial = strain_rows(g_all, gather_nodes(nodal_parts(res), onehots))
    product[...] = assemble(trial)


def unpack_kernel(place, *refs):
    msgs, (out, out_vmem, sems) = refs[:UNIT], refs[UNIT:]
    slot, size = place[0:1, :], place[1:2, :]
    order = lane_order()
    hots = [class_onehot(slot, size, c + 1) for c in range(NBMAX)]
    copies = []
    for a in range(NBMAX):
        pieces = []
        for c in range(a, NBMAX):
            lane0, row0 = CLASS_PLACE[c]
            lane = lane0 + LEVEL * a
            rows = jnp.concatenate([msgs[k][row0 : row0 + TILE, lane : lane + LEVEL] for k in range(UNIT)], axis=0)
            pieces.append(dot_nt(rows, order).astype(BF16))
        hot = jnp.concatenate(hots[a:], axis=0)
        out_vmem[a] = dot_tn(hot, jnp.concatenate(pieces, axis=0)).astype(BF16)
        copy = pltpu.make_async_copy(out_vmem.at[a], out.at[:, pl.ds(LEVEL * a, LEVEL)], sems.at[a])
        copy.start()
        copies.append(copy)
    for copy in copies:
        copy.wait()


def spec(space):
    return pl.BlockSpec(memory_space=space)


VM, SM, HB = pltpu.VMEM, pltpu.SMEM, pl.ANY


def call(kernel, args, spaces, outs, out_spaces, scratch):
    return pl.pallas_call(
        kernel,
        out_shape=[jax.ShapeDtypeStruct(s, d) for s, d in outs],
        in_specs=[spec(s) for s in spaces],
        out_specs=[spec(s) for s in out_spaces],
        scratch_shapes=scratch,
        compiler_params=pltpu.CompilerParams(vmem_limit_bytes=VMEM_LIMIT),
    )(*args)


def on_device(
    shape,
    displacement, nodal_load, connectivity, shape_grads, elem_volume, point_map, vol_blocks, c_affine,
    coupling, diag_blocks, diag_normal, off_blocks, off_row, off_col, off_normal, off_count, fluct_state,
):
    z_count = shape[2]
    groups = z_count * 4
    rounds = z_count // 2
    devices = 4 * groups
    elems = connectivity.shape[1]
    node_count = displacement.shape[1]
    index = {name: lax.axis_index(name) for name in AXES}
    unit_index = index["x"] * 4 + index["l"] * 2 + index["c"]
    ids = jnp.stack(
        [index["y"], index["x"], index["h"], index["l"], index["c"], unit_index, unit_index, unit_index]
    ).astype(I32)

    def coords(device):
        section, group = divmod(device, groups)
        return section // 2, section % 2, group // 4, (group // 2) % 2, group % 2

    def number(y, x, h, l, c):
        return (y * 2 + x) * groups + h * 4 + l * 2 + c

    def permute(value, source_of):
        pairs = [(number(*source_of(*coords(d))), d) for d in range(devices)]
        return lax.ppermute(value, AXES, pairs)

    def unit_permute(value, k):
        return permute(value, lambda y, x, h, l, c: (y, x ^ (k >> 2), h, l ^ ((k >> 1) & 1), c ^ (k & 1)))

    blocks, small, ints = call(
        matrix_pack_kernel,
        (
            ids, vol_blocks, off_row, off_col, off_count, coupling[:, 0], diag_normal[:, 0], off_normal[:, 0],
            c_affine[0], diag_blocks[:, 0], off_blocks[:, 0],
        ),
        (SM, SM, SM, SM, SM, VM, VM, VM, VM, HB, HB),
        (((HALF_ROWS + HALF_OFF, BS, BS), BF16), ((SM_ROWS, BS), F32), ((8, BS), I32)),
        (HB, VM, SM),
        [
            pltpu.SMEM((32,), I32), pltpu.SMEM((32,), I32), pltpu.SMEM((16,), I32), pltpu.SMEM((8,), I32),
            pltpu.SemaphoreType.DMA((HALF_ROWS + 1,)),
        ],
    )
    held = []
    for turn in range(rounds):
        def from_group(y, x, h, l, c, turn=turn):
            return y, x, (h + 2 * turn + (x ^ c)) % z_count, l, c

        mine = [permute(value, from_group) for value in (blocks, small, ints)]
        theirs = permute(mine[0][HALF_ROWS:], lambda y, x, h, l, c: (1 - y, x, h, l, c))
        held.append((mine[2], mine[1], mine[0], theirs))

    table = lax.all_to_all(
        jnp.broadcast_to(vol_blocks.astype(F32)[:, None, :], (groups, 1, VOL_GRP)),
        GROUP_AXES, split_axis=0, concat_axis=0, tiled=True,
    ).reshape(groups, VOL_GRP)
    packed = call(
        functools.partial(pack_kernel, groups, rounds),
        (ids, point_map.reshape(1, elems), table, displacement, connectivity, shape_grads, fluct_state),
        (SM, VM, VM, VM, VM, VM, HB),
        tuple(((2 * TILE, MSG_LANES), BF16) for _ in range(UNIT)) + (((8, elems), F32), ((8, elems), I32)),
        (VM,) * (UNIT + 2),
        [pltpu.VMEM((elems, NBMAX * LEVEL), BF16), pltpu.SemaphoreType.DMA],
    )
    strain, place = packed[UNIT:]
    msgs = [packed[0]] + [unit_permute(packed[k], k) for k in range(1, UNIT)]

    solved = None
    for turn in range(rounds):
        ints_t, small_t, blocks_t, other_t = held[turn]
        result = call(
            solve_kernel,
            (ids, ints_t, small_t, blocks_t, other_t, *msgs),
            (SM, SM) + (VM,) * (UNIT + 3),
            tuple(((2 * TILE, STATE_LANES), BF16) for _ in range(UNIT)) + (((UNIT, 2 * TILE, BS), BF16),),
            (VM,) * (UNIT + 1),
            [
                pltpu.VMEM((HALF_ROWS, COMPS * SLOTS, BS), F32),
                pltpu.VMEM((HALF_ROWS, COMPS * SLOTS, BS), BF16),
                pltpu.VMEM((HALF_ROWS, COMPS * SLOTS, BS), F32),
                pltpu.VMEM((OFF_GRP, SLOTS, BS), F32),
                pltpu.VMEM((HALF_ROWS, SLOTS, BS), F32),
                pltpu.VMEM((HALF_ROWS, SLOTS, BS), F32),
                pltpu.VMEM((NBMAX, SLOTS, BS), F32),
                pltpu.VMEM((HALF_ROWS // 2, 2 * BS, 2 * BS), BF16),
                pltpu.VMEM((OFF_GRP // 2, 2 * BS, 2 * BS), BF16),
            ],
        )
        if solved is None:
            solved = result
        else:
            of_turn = (jnp.arange(2 * TILE) % TILE) // (TILE // rounds) == turn
            solved = [jnp.where(of_turn[:, None], new, old) for new, old in zip(result, solved)]

    tangents = lax.all_to_all(solved[UNIT], UNIT_AXES, split_axis=0, concat_axis=0, tiled=True)
    back = [solved[0]] + [unit_permute(solved[k], k) for k in range(1, UNIT)]
    residual, product, norm = call(
        fem_kernel,
        (ids, tangents, place, strain, shape_grads, elem_volume.reshape(1, elems), connectivity, nodal_load),
        (SM,) + (VM,) * 7,
        (((3, node_count), F32), ((3, node_count), F32), ((devices, BS), F32)),
        (VM,) * 3,
        [],
    )
    norms = lax.all_to_all(norm, AXES, split_axis=0, concat_axis=0, tiled=True)
    norm_sq = jnp.sum(norms[:, 0])
    root_mean = jnp.sqrt(norm_sq / (3.0 * node_count * devices) + 1e-06)
    update = -jnp.minimum(1.0, CLIP_RMS / root_mean) * residual
    (fluct_new,) = call(
        unpack_kernel,
        (place, *back),
        (VM,) * (UNIT + 1),
        (((elems, NBMAX * LEVEL), BF16),),
        (HB,),
        [pltpu.VMEM((NBMAX, elems, LEVEL), BF16), pltpu.SemaphoreType.DMA((NBMAX,))],
    )
    return residual, product, update, fluct_new


def solution(mesh):
    sections, groups = mesh.shape["sec"], mesh.shape["bulk"]
    shape = (2, sections // 2, groups // 4, 2, 2)
    fine = Mesh(mesh.devices.reshape(shape), AXES)
    return jax.shard_map(
        functools.partial(on_device, shape),
        mesh=fine,
        in_specs=(
            P(None, AXES),
            P(None, AXES),
            P(None, AXES),
            P(None, AXES),
            P(AXES),
            P(AXES),
            P(GROUP_AXES, None),
            P(GROUP_AXES, None, None),
            P(None, GROUP_AXES, None, None),
            P(None, GROUP_AXES, None, None),
            P(None, GROUP_AXES, None),
            P(None, GROUP_AXES, None, None),
            P(None, GROUP_AXES),
            P(None, GROUP_AXES),
            P(None, GROUP_AXES, None),
            P(GROUP_AXES),
            P(AXES, None),
        ),
        out_specs=(P(None, AXES), P(None, AXES), P(None, AXES), P(AXES, None)),
        check_vma=False,
    )
```

```python
import functools

import jax
import jax.numpy as jnp
from jax import lax
from jax.experimental import pallas as pl
from jax.experimental.pallas import tpu as pltpu
from jax.sharding import Mesh, PartitionSpec as P

BS = 128
NBMAX = 4
VOL_GRP = 8
GPV_DEV = 64
SWEEPS = 3
ROWS_GRP = 20
HALF_ROWS = 10
OFF_GRP = 32
HALF_OFF = 16
COMPS = 6
LEVEL = BS * COMPS
UNIT = 8
TILE = 16
SLOTS = UNIT * TILE
STATE_LANES = 5 * LEVEL
MSG_LANES = STATE_LANES + 128
GAIN_NORMAL = 0.4
CLIP_RMS = 1.0
SM_NORMAL = 80
SM_AFFINE = 88
SM_ROWS = 96
RANK_LANE = 6

F32 = jnp.float32
BF16 = jnp.bfloat16
I32 = jnp.int32
AXES = ("y", "x", "h", "l", "c")
GROUP_AXES = ("h", "l", "c")
UNIT_AXES = ("x", "l", "c")
VMEM_LIMIT = 56 * 1024 * 1024

CLASS_PLACE = ((4 * LEVEL, 0), (3 * LEVEL, TILE), (0, TILE), (0, 0))
CLASS_BASE = (0, 1, 3, 6)


def dot_nn(lhs, rhs):
    return lax.dot_general(lhs, rhs, (((1,), (0,)), ((), ())), preferred_element_type=F32)


def dot_nt(lhs, rhs):
    return lax.dot_general(lhs, rhs, (((1,), (1,)), ((), ())), preferred_element_type=F32)


def dot_tn(lhs, rhs):
    return lax.dot_general(lhs, rhs, (((0,), (0,)), ((), ())), preferred_element_type=F32)


def split3(value):
    high = value.astype(BF16)
    rest = value - high.astype(F32)
    mid = rest.astype(BF16)
    low = (rest - mid.astype(F32)).astype(BF16)
    return high, mid, low


def iota(shape, dim):
    return lax.broadcasted_iota(I32, shape, dim)


def lane_order():
    target = iota((1, LEVEL), 1)
    source = COMPS * (target % BS) + target // BS
    return jnp.where(iota((LEVEL, LEVEL), 0) == source, 1.0, 0.0).astype(BF16)


def class_onehot(slot, size, level_rows):
    chosen = jnp.where(size == level_rows, slot, -1)
    return jnp.where(iota((SLOTS, slot.shape[1]), 0) == chosen, 1.0, 0.0).astype(BF16)


def returned_onehots(ids, tangents, slot, rank):
    packed, hots = [], [None] * NBMAX
    wanted = rank * SLOTS + slot
    place = iota((SLOTS, 1), 0)
    for row0, one, two in ((0, 3, 0), (TILE, 2, 1)):
        tile = jnp.concatenate([tangents[ids[5] ^ k, row0 : row0 + TILE, :] for k in range(UNIT)], axis=0)
        packed.append(tile)
        for c, lane in ((one, RANK_LANE), (two, 64 + RANK_LANE)):
            at = tile[:, lane : lane + 1].astype(F32).astype(I32) * SLOTS + place
            hots[c] = jnp.where(wanted == at, 1.0, 0.0).astype(BF16)
    return packed, hots


def node_onehot(conn_row, nodes):
    return jnp.where(iota((nodes, conn_row.shape[1]), 0) == conn_row, 1.0, 0.0).astype(BF16)


def nodal_parts(nodal):
    parts = [jnp.concatenate([p.astype(F32), jnp.zeros((13, p.shape[1]), F32)], axis=0) for p in split3(nodal)]
    rows = parts[0] + pltpu.roll(parts[1], 3, 0) + pltpu.roll(parts[2], 6, 0)
    return rows.astype(BF16)


def gather_nodes(rows, onehots):
    found = []
    for onehot in onehots:
        got = dot_nn(rows, onehot)
        found.append([got[i : i + 1] + got[i + 3 : i + 4] + got[i + 6 : i + 7] for i in range(3)])
    return found


def strain_rows(grads, disp):
    g = lambda a, k: grads[3 * a + k : 3 * a + k + 1]
    total = lambda f: f(0) + f(1) + f(2) + f(3)
    return [
        total(lambda a: g(a, 0) * disp[a][0]),
        total(lambda a: g(a, 1) * disp[a][1]),
        total(lambda a: g(a, 2) * disp[a][2]),
        total(lambda a: g(a, 2) * disp[a][1] + g(a, 1) * disp[a][2]),
        total(lambda a: g(a, 2) * disp[a][0] + g(a, 0) * disp[a][2]),
        total(lambda a: g(a, 1) * disp[a][0] + g(a, 0) * disp[a][1]),
    ]


def matrix_pack_kernel(
    ids, vol, off_row, off_col, off_count, coupling, diag_normal, off_normal, affine, diag, off,
    diag_out, off_out, small, ints, row_local, row_size, rows_sel, seen, sems,
):
    half = ids[0]
    off_copy = pltpu.make_async_copy(
        off.at[pl.ds(half * HALF_OFF, HALF_OFF)], off_out, sems.at[HALF_ROWS]
    )
    off_copy.start()
    small[...] = jnp.zeros_like(small)
    for size in range(NBMAX + 1):
        seen[size] = 0
    start = 0
    for v in range(VOL_GRP):
        size = vol[0, v]
        rank = seen[size]
        seen[size] = rank + 1
        mine = rank == half
        base = (size * (size - 1)) // 2
        for a in range(NBMAX):
            @pl.when(a < size)
            def _(a=a, size=size, base=base, mine=mine, start=start):
                row_local[start + a] = jnp.where(mine, base + a, -1)
                row_size[start + a] = size - 1

            @pl.when(jnp.logical_and(a < size, mine))
            def _(a=a, base=base, start=start):
                rows_sel[base + a] = start + a

        @pl.when(mine)
        def _(size=size, v=v):
            small[pl.ds(SM_AFFINE - 1 + size, 1), 0:36] = affine[v : v + 1, :]
            ints[6, size - 1] = v

        start = start + size
    copies = [off_copy]
    for i in range(HALF_ROWS):
        copies.append(
            pltpu.make_async_copy(diag.at[pl.ds(rows_sel[i], 1)], diag_out.at[pl.ds(i, 1)], sems.at[i])
        )
        copies[-1].start()
    lane = iota((8, BS), 1)
    normals = jnp.zeros((8, BS), F32)
    diag_rows = diag_normal[...]
    for i in range(HALF_ROWS):
        row = rows_sel[i]
        small[8 * i : 8 * i + COMPS, :] = coupling[pl.ds(COMPS * row, COMPS), :]
        normals += jnp.where(lane == i, pltpu.roll(diag_rows, (i - row + BS) % BS, 1), 0.0)
    off_rows = off_normal[...]
    direct = pltpu.roll(off_rows, HALF_OFF, 1)
    swapped = jnp.where(lane < 2 * HALF_OFF, off_rows, pltpu.roll(off_rows, 2 * HALF_OFF, 1))
    chosen = jnp.where(half == 0, direct, swapped)
    normals += jnp.where(jnp.logical_and(lane >= HALF_OFF, lane < HALF_OFF + OFF_GRP), chosen, 0.0)
    small[SM_NORMAL : SM_NORMAL + 8, :] = normals
    live_total = off_count[0]

    def contact(n, found):
        slot = (n + half * HALF_OFF) % OFF_GRP
        row = off_row[0, slot]
        local = row_local[row]
        ints[5, n] = row_size[row]
        live = jnp.logical_and(slot < live_total, local >= 0)

        @pl.when(live)
        def _():
            ints[1, found] = n
            ints[2, found] = local
            ints[3, found] = row_local[off_col[0, slot]]

        return found + live.astype(I32)

    ints[0, 0] = lax.fori_loop(0, OFF_GRP, contact, 0)
    for copy in copies:
        copy.wait()


def pack_kernel(groups, rounds, ids, point_map, disp, conn, grads, state, *refs):
    out, strain_out, place_out, state_vmem, sem = refs
    load = pltpu.make_async_copy(state, state_vmem, sem)
    load.start()
    elems = point_map.shape[1]
    x_me, h_me, l_me, c_me = ids[1], ids[2], ids[3], ids[4]
    z_count = groups // 4
    codes = point_map[...]
    owner = codes // elems
    within = codes % elems
    group = owner % groups
    volume = within // GPV_DEV
    delta = (group // 4 - h_me + z_count) % z_count
    core = group % 2
    low = (group // 2) % 2
    across = (delta % 2) ^ core
    turn = delta // 2
    offset = ((across ^ x_me) * 4) + ((low ^ l_me) * 2) + (core ^ c_me)
    volumes = groups * VOL_GRP
    volume_hot = iota((volumes, elems), 0) == group * VOL_GRP + volume
    volume_hot16 = jnp.where(volume_hot, 1.0, 0.0).astype(BF16)
    load.wait()
    ones = jnp.ones((8, LEVEL), BF16)
    filled = jnp.concatenate(
        [dot_nt(ones, jnp.abs(state_vmem[:, LEVEL * a : LEVEL * (a + 1)]))[0:1] for a in range(NBMAX)], axis=0
    )
    marks = jnp.concatenate(
        [jnp.where(filled > 0.0, 1.0, 0.0), jnp.ones((1, elems), F32), jnp.zeros((3, elems), F32)], axis=0
    ).astype(BF16)

    def code_of(take, counts, number):
        height = jnp.zeros_like(number)
        for a in range(NBMAX):
            height = jnp.where(take(counts, a) > 0.0, a + 1, height)
        return jnp.where(take(counts, NBMAX) > 0.0, height * VOL_GRP + number % VOL_GRP, 1 << 20)

    code_row = code_of(
        lambda x, a: x[a : a + 1, :], dot_nt(marks, volume_hot16), iota((1, volumes), 1)
    )
    code_col = code_of(
        lambda x, a: x[:, a : a + 1], dot_nt(volume_hot16, marks), iota((volumes, 1), 0)
    )
    same = iota((volumes, volumes), 0) // VOL_GRP == iota((volumes, volumes), 1) // VOL_GRP
    below = jnp.where(jnp.logical_and(same, code_row < code_col), 1, 0)
    rank_col = jnp.sum(below, axis=1, keepdims=True) + 1
    size = jnp.sum(jnp.where(volume_hot, rank_col, 0), axis=0, keepdims=True)
    key = (offset * NBMAX + size - 1) * rounds + turn
    key_hot = iota((UNIT * NBMAX * rounds, elems), 0) == key
    earlier = jnp.where(iota((elems, elems), 0) < iota((elems, elems), 1), 1.0, 0.0).astype(BF16)
    counts = dot_nn(jnp.where(key_hot, 1.0, 0.0).astype(BF16), earlier)
    rank = jnp.sum(jnp.where(key_hot, counts, 0.0), axis=0, keepdims=True).astype(I32)
    slot = offset * TILE + turn * (TILE // rounds) + rank
    place_out[...] = jnp.concatenate([slot, size, jnp.zeros((6, elems), I32)], axis=0)

    nodes = disp.shape[1]
    onehots = [node_onehot(conn[a : a + 1, :], nodes) for a in range(4)]
    found = gather_nodes(nodal_parts(disp[...]), onehots)
    strain = strain_rows(grads[...], found)
    strain8 = jnp.concatenate(strain + [volume.astype(F32), jnp.zeros((1, elems), F32)], axis=0)
    strain_out[...] = strain8
    first = jnp.concatenate([strain8, jnp.zeros((120, elems), F32)], axis=0).astype(BF16)
    second = jnp.concatenate(
        [jnp.zeros((64, elems), F32), strain8, jnp.zeros((56, elems), F32)], axis=0
    ).astype(BF16)
    hots = [class_onehot(slot, size, c + 1) for c in range(NBMAX)]
    for one, other, row0 in ((3, 0, 0), (2, 1, TILE)):
        extras = (dot_nt(hots[one], first) + dot_nt(hots[other], second)).astype(BF16)
        for k in range(UNIT):
            out[ids[5] ^ k, row0 : row0 + TILE, STATE_LANES:] = extras[TILE * k : TILE * (k + 1)]
    order = lane_order()
    for c in range(NBMAX):
        lane0, row0 = CLASS_PLACE[c]
        for a in range(c + 1):
            rows = dot_nn(hots[c], state_vmem[:, LEVEL * a : LEVEL * (a + 1)]).astype(BF16)
            rows = dot_nn(rows, order).astype(BF16)
            for k in range(UNIT):
                out[ids[5] ^ k, row0 : row0 + TILE, lane0 + LEVEL * a : lane0 + LEVEL * (a + 1)] = rows[
                    TILE * k : TILE * (k + 1)
                ]


def solve_kernel(ids, ints, small, blocks, own, other, msgs, *refs):
    outs, refs = refs[:UNIT], refs[UNIT:]
    tangents, state, low, acc, contact_scale, diag_scale, inverse, response, diag_pairs, off_pairs = refs
    extras = []
    for rank in range(NBMAX):
        row0 = CLASS_PLACE[rank][1]
        tile = jnp.concatenate([msgs[ids[5] ^ k, row0 : row0 + TILE, STATE_LANES:] for k in range(UNIT)], axis=0).astype(F32)
        extras.append(tile if rank >= 2 else pltpu.roll(tile, 64, 1))
    held = [[extras[rank][:, RANK_LANE : RANK_LANE + 1] == ints[6, c].astype(F32) for rank in range(NBMAX)] for c in range(NBMAX)]
    agree = functools.reduce(jnp.logical_and, [held[c][c] for c in range(NBMAX)])
    in_order = jnp.min(jnp.where(agree, 1.0, 0.0)) > 0.5

    @pl.when(in_order)
    def _():
        for c in range(NBMAX):
            lane0, row0 = CLASS_PLACE[c]
            for a in range(c + 1):
                r = CLASS_BASE[c] + a
                for j in range(COMPS):
                    lane = lane0 + LEVEL * a + BS * j
                    for k in range(UNIT):
                        piece = msgs[ids[5] ^ k, row0 : row0 + TILE, lane : lane + BS]
                        dst = slice(SLOTS * j + TILE * k, SLOTS * j + TILE * (k + 1))
                        low[r, dst, :] = piece
                        state[r, dst, :] = piece.astype(F32)

    @pl.when(jnp.logical_not(in_order))
    def _():
        def component(j, carry):
            for c in range(NBMAX):
                for a in range(c + 1):
                    r = CLASS_BASE[c] + a
                    total = jnp.zeros((SLOTS, BS), F32)
                    for rank in range(a, NBMAX):
                        lane0, row0 = CLASS_PLACE[rank]
                        lane = pl.multiple_of(lane0 + LEVEL * a + BS * j, BS)
                        piece = jnp.concatenate(
                            [msgs[ids[5] ^ k, row0 : row0 + TILE, pl.ds(lane, BS)] for k in range(UNIT)], axis=0
                        )
                        total = jnp.where(held[c][rank], piece.astype(F32), total)
                    dst = pl.ds(pl.multiple_of(SLOTS * j, SLOTS), SLOTS)
                    low[r, dst, :] = total.astype(BF16)
                    state[r, dst, :] = total
            return carry

        lax.fori_loop(0, COMPS, component, 0)

    normals = small[SM_NORMAL : SM_NORMAL + 8, :]
    normals = jnp.concatenate([normals, jnp.zeros((BS - 8, BS), F32)], axis=0)
    parts = split3(normals)
    for c in range(NBMAX):
        strains = jnp.zeros((SLOTS, BS), F32)
        for rank in range(NBMAX):
            strains = jnp.where(held[c][rank], extras[rank], strains)
        strains = strains.astype(BF16)
        dots = dot_nn(strains, parts[0]) + dot_nn(strains, parts[1]) + dot_nn(strains, parts[2])
        response[c] = 1.0 + GAIN_NORMAL * jnp.tanh(dots)
    eye = iota((BS, BS), 0) == iota((BS, BS), 1)
    for c in range(NBMAX):
        for a in range(c + 1):
            r = CLASS_BASE[c] + a
            scale = jnp.broadcast_to(response[c, :, r : r + 1], (SLOTS, BS))
            diag_scale[r] = scale
            values = jnp.sum(jnp.where(eye, blocks[r].astype(F32), 0.0), axis=0, keepdims=True)
            inverse[r] = 1.0 / (scale * values)
    for n in range(OFF_GRP):
        contact_scale[n] = jnp.broadcast_to(
            response[ints[5, n], :, HALF_OFF + n : HALF_OFF + n + 1], (SLOTS, BS)
        )
    zero = jnp.zeros((BS, BS), BF16)
    for p in range(HALF_ROWS // 2):
        diag_pairs[p, :BS, :BS] = blocks[2 * p]
        diag_pairs[p, :BS, BS:] = zero
        diag_pairs[p, BS:, :BS] = zero
        diag_pairs[p, BS:, BS:] = blocks[2 * p + 1]
    live = ints[0, 0]
    pairs = (live + 1) // 2

    def contact_block(n):
        mine = n < HALF_OFF
        return jnp.where(mine, own[jnp.where(mine, n, 0)], other[jnp.where(mine, 0, n - HALF_OFF)])

    def fill(p, carry):
        off_pairs[p, :BS, :BS] = contact_block(ints[1, 2 * p])
        off_pairs[p, :BS, BS:] = zero
        off_pairs[p, BS:, :BS] = zero
        has_second = 2 * p + 1 < live

        @pl.when(has_second)
        def _():
            off_pairs[p, BS:, BS:] = contact_block(ints[1, 2 * p + 1])

        @pl.when(jnp.logical_not(has_second))
        def _():
            off_pairs[p, BS:, BS:] = zero

        return carry

    lax.fori_loop(0, pairs, fill, 0)

    def sweep(step, carry):
        for p in range(HALF_ROWS // 2):
            both = jnp.concatenate([low[2 * p], low[2 * p + 1]], axis=1)
            product = dot_nt(both, diag_pairs[p])
            for i in range(2):
                r = 2 * p + i
                scale = diag_scale[r]
                for j in range(COMPS):
                    rows = slice(SLOTS * j, SLOTS * (j + 1))
                    acc[r, rows, :] = product[rows, BS * i : BS * (i + 1)] * scale

        def contact(p, inner):
            second = jnp.minimum(2 * p + 1, live - 1)
            slots = (2 * p, second)
            both = jnp.concatenate([low[ints[3, m]] for m in slots], axis=1)
            product = dot_nt(both, off_pairs[p])
            for i, m in enumerate(slots):
                r = ints[2, m]
                scale = contact_scale[ints[1, m]]
                for j in range(COMPS):
                    rows = slice(SLOTS * j, SLOTS * (j + 1))
                    acc[r, rows, :] += product[rows, BS * i : BS * (i + 1)] * scale
            return inner

        lax.fori_loop(0, pairs, contact, 0)
        for r in range(HALF_ROWS):
            inv = inverse[r]
            for j in range(COMPS):
                rows = slice(SLOTS * j, SLOTS * (j + 1))
                load = small[8 * r + j : 8 * r + j + 1, :]
                value = state[r, rows, :] + (load - acc[r, rows, :]) * inv
                state[r, rows, :] = value
                low[r, rows, :] = value.astype(BF16)
        return carry

    lax.fori_loop(0, SWEEPS, sweep, 0)
    lane = iota((1, BS), 1)
    comp = lane // 8
    for c in range(NBMAX):
        total = jnp.zeros((SLOTS, BS), F32)
        for a in range(c + 1):
            r = CLASS_BASE[c] + a
            load8 = small[8 * r : 8 * r + 8, :]
            tiled = jnp.concatenate([load8] * 6 + [jnp.zeros((80, BS), F32)], axis=0)
            weights = jnp.concatenate(split3(tiled)[:2], axis=0)
            value = state[r]
            high = value.astype(BF16)
            rest = (value - high.astype(F32)).astype(BF16)
            product = dot_nt(high, weights) + dot_nt(rest, weights)
            product = product[:, :BS] + product[:, BS:]
            for j in range(COMPS):
                total += jnp.where(comp == j, product[SLOTS * j : SLOTS * (j + 1)], 0.0)
        source = iota((BS, BS), 0)
        target = iota((BS, BS), 1)
        wanted = jnp.logical_and(
            source == 6 * (target % 8) + target // 8, jnp.logical_and(target % 8 < 6, target < 48)
        )
        moved = jnp.sum(
            jnp.where(wanted, jnp.transpose(jnp.broadcast_to(small[SM_AFFINE + c : SM_AFFINE + c + 1, :], (BS, BS))), 0.0),
            axis=0,
            keepdims=True,
        )
        found = sum(jnp.where(held[c][rank], rank + 1.0, 0.0) for rank in range(NBMAX))
        acc[c, :SLOTS, :] = jnp.where(lane == RANK_LANE, found, moved - total / ((c + 1) * BS))
    for row0, one, two in ((0, 3, 0), (TILE, 2, 1)):
        first = acc[one, :SLOTS, :]
        second = acc[two, :SLOTS, :]
        packed = jnp.where(lane < 64, first, pltpu.roll(second, 64, 1)).astype(BF16)
        for k in range(UNIT):
            tangents[ids[5] ^ k, row0 : row0 + TILE, :] = packed[TILE * k : TILE * (k + 1)]
    for c in range(NBMAX):
        lane0, row0 = CLASS_PLACE[c]
        for a in range(c + 1):
            r = CLASS_BASE[c] + a
            for j in range(COMPS):
                lane_at = lane0 + LEVEL * a + BS * j
                for k in range(UNIT):
                    outs[k][row0 : row0 + TILE, lane_at : lane_at + BS] = low[
                        r, SLOTS * j + TILE * k : SLOTS * j + TILE * (k + 1), :
                    ]


def fem_kernel(ids, tangents, place, strain, grads, volume, conn, nodal_load, residual, product, norm):
    elems = place.shape[1]
    nodes = nodal_load.shape[1]
    slot, size = place[0:1, :], place[1:2, :]
    packed, hots = returned_onehots(ids, tangents, slot, size)
    entries = jnp.zeros((64, elems), F32)
    for tile, one, two in ((packed[0], 3, 0), (packed[1], 2, 1)):
        entries += dot_tn(tile, hots[one])[:64]
        entries += dot_tn(tile, hots[two])[64:]
    entry = lambda i, j: entries[8 * j + i : 8 * j + i + 1]
    weight = volume[...]
    g_all = grads[...]
    g = lambda a, k: g_all[3 * a + k : 3 * a + k + 1]
    onehots = [node_onehot(conn[a : a + 1, :], nodes) for a in range(4)]

    def assemble(strains):
        s = []
        for i in range(COMPS):
            total = entry(i, 0) * strains[0]
            for j in range(1, COMPS):
                total = total + entry(i, j) * strains[j]
            s.append(total * weight)
        result = jnp.zeros((TILE, nodes), F32)
        for a in range(4):
            force = jnp.concatenate(
                [
                    g(a, 0) * s[0] + g(a, 2) * s[4] + g(a, 1) * s[5],
                    g(a, 1) * s[1] + g(a, 2) * s[3] + g(a, 0) * s[5],
                    g(a, 2) * s[2] + g(a, 1) * s[3] + g(a, 0) * s[4],
                ],
                axis=0,
            )
            result += dot_nt(nodal_parts(force), onehots[a])
        return result[0:3] + result[3:6] + result[6:9]

    strains = strain[...]
    res = assemble([strains[i : i + 1] for i in range(COMPS)]) - nodal_load[...]
    residual[...] = res
    norm[...] = jnp.broadcast_to(jnp.sum(res * res, keepdims=True), norm.shape)
    trial = strain_rows(g_all, gather_nodes(nodal_parts(res), onehots))
    product[...] = assemble(trial)


def unpack_kernel(ids, place, tangents, *refs):
    msgs, (out, out_vmem, sems) = refs[:UNIT], refs[UNIT:]
    slot, size = place[0:1, :], place[1:2, :]
    order = lane_order()
    hots = returned_onehots(ids, tangents, slot, size)[1]
    copies = []
    for a in range(NBMAX):
        pieces = []
        for c in range(a, NBMAX):
            lane0, row0 = CLASS_PLACE[c]
            lane = lane0 + LEVEL * a
            rows = jnp.concatenate([msgs[k][row0 : row0 + TILE, lane : lane + LEVEL] for k in range(UNIT)], axis=0)
            pieces.append(dot_nt(rows, order).astype(BF16))
        hot = jnp.concatenate(hots[a:], axis=0)
        out_vmem[a] = dot_tn(hot, jnp.concatenate(pieces, axis=0)).astype(BF16)
        copy = pltpu.make_async_copy(out_vmem.at[a], out.at[:, pl.ds(LEVEL * a, LEVEL)], sems.at[a])
        copy.start()
        copies.append(copy)
    for copy in copies:
        copy.wait()


def spec(space):
    return pl.BlockSpec(memory_space=space)


VM, SM, HB = pltpu.VMEM, pltpu.SMEM, pl.ANY


def call(kernel, args, spaces, outs, out_spaces, scratch):
    return pl.pallas_call(
        kernel,
        out_shape=[jax.ShapeDtypeStruct(s, d) for s, d in outs],
        in_specs=[spec(s) for s in spaces],
        out_specs=[spec(s) for s in out_spaces],
        scratch_shapes=scratch,
        compiler_params=pltpu.CompilerParams(vmem_limit_bytes=VMEM_LIMIT),
    )(*args)


def solve_call(*args):
    return call(
        solve_kernel,
        args,
        (SM, SM) + (VM,) * 5,
        tuple(((2 * TILE, STATE_LANES), BF16) for _ in range(UNIT)) + (((UNIT, 2 * TILE, BS), BF16),),
        (VM,) * (UNIT + 1),
        [
            pltpu.VMEM((HALF_ROWS, COMPS * SLOTS, BS), F32),
            pltpu.VMEM((HALF_ROWS, COMPS * SLOTS, BS), BF16),
            pltpu.VMEM((HALF_ROWS, COMPS * SLOTS, BS), F32),
            pltpu.VMEM((OFF_GRP, SLOTS, BS), F32),
            pltpu.VMEM((HALF_ROWS, SLOTS, BS), F32),
            pltpu.VMEM((HALF_ROWS, SLOTS, BS), F32),
            pltpu.VMEM((NBMAX, SLOTS, BS), F32),
            pltpu.VMEM((HALF_ROWS // 2, 2 * BS, 2 * BS), BF16),
            pltpu.VMEM((OFF_GRP // 2, 2 * BS, 2 * BS), BF16),
        ],
    )


def pack_call(groups, rounds, *args):
    elems = args[1].shape[1]
    return call(
        functools.partial(pack_kernel, groups, rounds),
        args,
        (SM, VM, VM, VM, VM, HB),
        (((UNIT, 2 * TILE, MSG_LANES), BF16), ((8, elems), F32), ((8, elems), I32)),
        (VM,) * 3,
        [pltpu.VMEM((elems, NBMAX * LEVEL), BF16), pltpu.SemaphoreType.DMA],
    )


def unpack_call(*args):
    elems = args[1].shape[1]
    return call(
        unpack_kernel,
        args,
        (SM,) + (VM,) * (UNIT + 2),
        (((elems, NBMAX * LEVEL), BF16),),
        (HB,),
        [pltpu.VMEM((NBMAX, elems, LEVEL), BF16), pltpu.SemaphoreType.DMA((NBMAX,))],
    )


def on_device(
    shape,
    displacement, nodal_load, connectivity, shape_grads, elem_volume, point_map, vol_blocks, c_affine,
    coupling, diag_blocks, diag_normal, off_blocks, off_row, off_col, off_normal, off_count, fluct_state,
):
    z_count = shape[2]
    groups = z_count * 4
    rounds = z_count // 2
    devices = 4 * groups
    elems = connectivity.shape[1]
    node_count = displacement.shape[1]
    index = {name: lax.axis_index(name) for name in AXES}
    unit_index = index["x"] * 4 + index["l"] * 2 + index["c"]
    ids = jnp.stack(
        [index["y"], index["x"], index["h"], index["l"], index["c"], unit_index, unit_index, unit_index]
    ).astype(I32)

    def coords(device):
        section, group = divmod(device, groups)
        return section // 2, section % 2, group // 4, (group // 2) % 2, group % 2

    def number(y, x, h, l, c):
        return (y * 2 + x) * groups + h * 4 + l * 2 + c

    def permute(value, source_of):
        pairs = [(number(*source_of(*coords(d))), d) for d in range(devices)]
        return lax.ppermute(value, AXES, pairs)

    def unit_permute(value, k):
        return permute(value, lambda y, x, h, l, c: (y, x ^ (k >> 2), h, l ^ ((k >> 1) & 1), c ^ (k & 1)))

    def normal_rows(normals):
        return jnp.pad(normals.transpose(2, 1, 0)[:, 0], ((0, 2), (0, BS - normals.shape[0])))

    diag_half, off_half, small, ints = call(
        matrix_pack_kernel,
        (
            ids, vol_blocks, off_row.T, off_col.T, off_count, coupling.reshape(ROWS_GRP * COMPS, BS),
            normal_rows(diag_normal), normal_rows(off_normal), c_affine[0], diag_blocks[:, 0], off_blocks[:, 0],
        ),
        (SM, SM, SM, SM, SM, VM, VM, VM, VM, HB, HB),
        (((HALF_ROWS, BS, BS), BF16), ((HALF_OFF, BS, BS), BF16), ((SM_ROWS, BS), F32), ((8, BS), I32)),
        (VM, VM, VM, SM),
        [
            pltpu.SMEM((32,), I32), pltpu.SMEM((32,), I32), pltpu.SMEM((16,), I32), pltpu.SMEM((8,), I32),
            pltpu.SemaphoreType.DMA((HALF_ROWS + 1,)),
        ],
    )
    packed, strain, place = pack_call(
        groups, rounds, ids, point_map.reshape(1, elems), displacement, connectivity, shape_grads, fluct_state
    )
    msgs = lax.all_to_all(packed, UNIT_AXES, split_axis=0, concat_axis=0, tiled=True)

    solved = None
    for turn in range(rounds):
        def from_group(y, x, h, l, c, turn=turn):
            return y, x, (h + 2 * turn + (x ^ c)) % z_count, l, c

        mine_t, diag_t, small_t, ints_t = lax.optimization_barrier(
            tuple(permute(value, from_group) for value in (off_half, diag_half, small, ints))
        )
        other_t = permute(mine_t, lambda y, x, h, l, c: (1 - y, x, h, l, c))
        result = solve_call(ids, ints_t, small_t, diag_t, mine_t, other_t, msgs)
        if solved is None:
            solved = result
        else:
            of_turn = (jnp.arange(2 * TILE) % TILE) // (TILE // rounds) == turn
            solved = [jnp.where(of_turn[:, None], new, old) for new, old in zip(result, solved)]

    back = [solved[0]] + [unit_permute(solved[k], k) for k in range(1, UNIT)]
    own, back[4] = lax.optimization_barrier((solved[UNIT], back[4]))
    tangents = lax.all_to_all(own, UNIT_AXES, split_axis=0, concat_axis=0, tiled=True)
    residual, product, norm = call(
        fem_kernel,
        (ids, tangents, place, strain, shape_grads, elem_volume.reshape(1, elems), connectivity, nodal_load),
        (SM,) + (VM,) * 7,
        (((3, node_count), F32), ((3, node_count), F32), ((devices, BS), F32)),
        (VM,) * 3,
        [],
    )
    norms = lax.all_to_all(norm, AXES, split_axis=0, concat_axis=0, tiled=True)
    norm_sq = jnp.sum(norms[:, 0])
    root_mean = jnp.sqrt(norm_sq / (3.0 * node_count * devices) + 1e-06)
    update = -jnp.minimum(1.0, CLIP_RMS / root_mean) * residual
    (fluct_new,) = unpack_call(ids, place, tangents, *back)
    return residual, product, update, fluct_new


def solution(mesh):
    sections, groups = mesh.shape["sec"], mesh.shape["bulk"]
    shape = (2, sections // 2, groups // 4, 2, 2)
    fine = Mesh(mesh.devices.reshape(shape), AXES)
    return jax.shard_map(
        functools.partial(on_device, shape),
        mesh=fine,
        in_specs=(
            P(None, AXES),
            P(None, AXES),
            P(None, AXES),
            P(None, AXES),
            P(AXES),
            P(AXES),
            P(GROUP_AXES, None),
            P(GROUP_AXES, None, None),
            P(None, GROUP_AXES, None, None),
            P(None, GROUP_AXES, None, None),
            P(None, GROUP_AXES, None),
            P(None, GROUP_AXES, None, None),
            P(None, GROUP_AXES),
            P(None, GROUP_AXES),
            P(None, GROUP_AXES, None),
            P(GROUP_AXES),
            P(AXES, None),
        ),
        out_specs=(P(None, AXES), P(None, AXES), P(None, AXES), P(AXES, None)),
        check_vma=False,
    )
```

```python
import functools

import jax
import jax.numpy as jnp
from jax import lax
from jax.experimental import pallas as pl
from jax.experimental.pallas import tpu as pltpu
from jax.sharding import Mesh, PartitionSpec as P

BS = 128
NBMAX = 4
VOL_GRP = 8
GPV_DEV = 64
SWEEPS = 3
ROWS_GRP = 20
HALF_ROWS = 10
OFF_GRP = 32
HALF_OFF = 16
COMPS = 6
LEVEL = BS * COMPS
UNIT = 8
TILE = 16
SLOTS = UNIT * TILE
STATE_LANES = 5 * LEVEL
MSG_LANES = STATE_LANES + 128
GAIN_NORMAL = 0.4
WIDE = 8
CHUNK = 256
CLIP_RMS = 1.0
SM_NORMAL = 80
SM_AFFINE = 88
SM_ROWS = 96
RANK_LANE = 6

F32 = jnp.float32
BF16 = jnp.bfloat16
I32 = jnp.int32
AXES = ("y", "x", "h", "l", "c")
GROUP_AXES = ("h", "l", "c")
UNIT_AXES = ("x", "l", "c")
VMEM_LIMIT = 56 * 1024 * 1024

CLASS_PLACE = ((4 * LEVEL, 0), (3 * LEVEL, TILE), (0, TILE), (0, 0))
CLASS_BASE = (0, 1, 3, 6)


def dot_nn(lhs, rhs):
    return lax.dot_general(lhs, rhs, (((1,), (0,)), ((), ())), preferred_element_type=F32)


def dot_nt(lhs, rhs):
    return lax.dot_general(lhs, rhs, (((1,), (1,)), ((), ())), preferred_element_type=F32)


def dot_tn(lhs, rhs):
    return lax.dot_general(lhs, rhs, (((0,), (0,)), ((), ())), preferred_element_type=F32)


def split3(value):
    high = value.astype(BF16)
    rest = value - high.astype(F32)
    mid = rest.astype(BF16)
    low = (rest - mid.astype(F32)).astype(BF16)
    return high, mid, low


def iota(shape, dim):
    return lax.broadcasted_iota(I32, shape, dim)


def lane_order():
    target = iota((1, LEVEL), 1)
    source = COMPS * (target % BS) + target // BS
    return jnp.where(iota((LEVEL, LEVEL), 0) == source, 1.0, 0.0).astype(BF16)


def lane_order_back():
    row = iota((LEVEL, 1), 0)
    return jnp.where(iota((LEVEL, LEVEL), 1) == COMPS * (row % BS) + row // BS, 1.0, 0.0).astype(BF16)


def class_onehot(slot, size, level_rows):
    chosen = jnp.where(size == level_rows, slot, -1)
    return jnp.where(iota((SLOTS, slot.shape[1]), 0) == chosen, 1.0, 0.0).astype(BF16)


def returned_onehots(ids, tangents, slot, rank):
    packed, hots = [], [None] * NBMAX
    wanted = rank * SLOTS + slot
    place = iota((SLOTS, 1), 0)
    for row0, one, two in ((0, 3, 0), (TILE, 2, 1)):
        tile = jnp.concatenate([tangents[ids[5] ^ k, row0 : row0 + TILE, :] for k in range(UNIT)], axis=0)
        packed.append(tile)
        for c, lane in ((one, RANK_LANE), (two, 64 + RANK_LANE)):
            at = tile[:, lane : lane + 1].astype(F32).astype(I32) * SLOTS + place
            hots[c] = jnp.where(wanted == at, 1.0, 0.0).astype(BF16)
    return packed, hots


def node_onehot(conn_row, nodes):
    return jnp.where(iota((nodes, conn_row.shape[1]), 0) == conn_row, 1.0, 0.0).astype(BF16)


def nodal_parts(nodal):
    parts = [jnp.concatenate([p.astype(F32), jnp.zeros((13, p.shape[1]), F32)], axis=0) for p in split3(nodal)]
    rows = parts[0] + pltpu.roll(parts[1], 3, 0) + pltpu.roll(parts[2], 6, 0)
    return rows.astype(BF16)


def gather_nodes(rows, onehots):
    found = []
    for onehot in onehots:
        got = dot_nn(rows, onehot)
        found.append([got[i : i + 1] + got[i + 3 : i + 4] + got[i + 6 : i + 7] for i in range(3)])
    return found


def strain_rows(grads, disp):
    g = lambda a, k: grads[3 * a + k : 3 * a + k + 1]
    total = lambda f: f(0) + f(1) + f(2) + f(3)
    return [
        total(lambda a: g(a, 0) * disp[a][0]),
        total(lambda a: g(a, 1) * disp[a][1]),
        total(lambda a: g(a, 2) * disp[a][2]),
        total(lambda a: g(a, 2) * disp[a][1] + g(a, 1) * disp[a][2]),
        total(lambda a: g(a, 2) * disp[a][0] + g(a, 0) * disp[a][2]),
        total(lambda a: g(a, 1) * disp[a][0] + g(a, 0) * disp[a][1]),
    ]


def matrix_pack_kernel(
    ids, vol, off_row, off_col, off_count, coupling, diag_normal, off_normal, affine, diag,
    diag_out, small, ints, row_local, row_size, rows_sel, seen, sems,
):
    half = ids[0]
    small[...] = jnp.zeros_like(small)
    small[0:VOL_GRP, 0:36] = affine[...]
    target = iota((1, BS), 1) % 64
    source = jnp.where(jnp.logical_and(target % 8 < 6, target < 48), 6 * (target % 8) + target // 8, -1)
    shift = jnp.where(iota((BS, BS), 0) == source, 1.0, 0.0).astype(BF16)
    moved = sum(dot_nn(part, shift) for part in split3(small[0:VOL_GRP, :]))
    small[0:VOL_GRP, :] = jnp.zeros((VOL_GRP, BS), F32)
    for size in range(NBMAX + 1):
        seen[size] = 0
    start = 0
    for v in range(VOL_GRP):
        size = vol[0, v]
        rank = seen[size]
        seen[size] = rank + 1
        mine = rank == half
        base = (size * (size - 1)) // 2
        for a in range(NBMAX):
            @pl.when(a < size)
            def _(a=a, size=size, base=base, mine=mine, start=start):
                row_local[start + a] = jnp.where(mine, base + a, -1)
                row_size[start + a] = size - 1

            @pl.when(jnp.logical_and(a < size, mine))
            def _(a=a, base=base, start=start):
                rows_sel[base + a] = start + a

        @pl.when(mine)
        def _(size=size, v=v):
            small[pl.ds(SM_AFFINE - 1 + size, 1), :] = moved[v : v + 1, :]
            ints[6, size - 1] = v

        start = start + size
    copies = []
    for i in range(HALF_ROWS):
        copies.append(
            pltpu.make_async_copy(diag.at[pl.ds(rows_sel[i], 1)], diag_out.at[pl.ds(i, 1)], sems.at[i])
        )
        copies[-1].start()
    lane = iota((8, BS), 1)
    normals = jnp.zeros((8, BS), F32)
    diag_rows = diag_normal[...]
    for i in range(HALF_ROWS):
        row = rows_sel[i]
        small[8 * i : 8 * i + COMPS, :] = coupling[pl.ds(COMPS * row, COMPS), :]
        normals += jnp.where(lane == i, pltpu.roll(diag_rows, (i - row + BS) % BS, 1), 0.0)
    normals += pltpu.roll(off_normal[...], HALF_OFF, 1)
    small[SM_NORMAL : SM_NORMAL + 8, :] = normals
    live_total = off_count[0]

    def contact(n, found):
        row = off_row[0, n]
        local = row_local[row]
        ints[4, n] = jnp.maximum(local, 0)
        ints[5, n] = row_size[row]
        live = jnp.logical_and(n < live_total, local >= 0)

        @pl.when(live)
        def _():
            ints[1, found] = n
            ints[2, found] = local
            ints[3, found] = row_local[off_col[0, n]]

        return found + live.astype(I32)

    ints[0, 0] = lax.fori_loop(0, OFF_GRP, contact, 0)
    for copy in copies:
        copy.wait()


def pack_kernel(groups, rounds, ids, point_map, disp, conn, grads, state, *refs):
    out, strain_out, place_out, state_vmem, sem = refs
    load = pltpu.make_async_copy(state, state_vmem, sem)
    load.start()
    elems = point_map.shape[1]
    x_me, h_me, l_me, c_me = ids[1], ids[2], ids[3], ids[4]
    z_count = groups // 4
    codes = point_map[...]
    owner = codes // elems
    within = codes % elems
    group = owner % groups
    volume = within // GPV_DEV
    delta = (group // 4 - h_me + z_count) % z_count
    core = group % 2
    low = (group // 2) % 2
    across = (delta % 2) ^ core
    turn = delta // 2
    offset = ((across ^ x_me) * 4) + ((low ^ l_me) * 2) + (core ^ c_me)
    volumes = groups * VOL_GRP
    volume_hot = iota((volumes, elems), 0) == group * VOL_GRP + volume
    volume_hot16 = jnp.where(volume_hot, 1.0, 0.0).astype(BF16)
    load.wait()
    ones = jnp.ones((8, LEVEL), BF16)
    filled = jnp.concatenate(
        [dot_nt(ones, jnp.abs(state_vmem[:, LEVEL * a : LEVEL * (a + 1)]))[0:1] for a in range(NBMAX)], axis=0
    )
    marks = jnp.concatenate(
        [jnp.where(filled > 0.0, 1.0, 0.0), jnp.ones((1, elems), F32), jnp.zeros((3, elems), F32)], axis=0
    ).astype(BF16)

    def code_of(take, counts, number):
        height = jnp.zeros_like(number)
        for a in range(NBMAX):
            height = jnp.where(take(counts, a) > 0.0, a + 1, height)
        return jnp.where(take(counts, NBMAX) > 0.0, height * VOL_GRP + number % VOL_GRP, 1 << 20)

    code_row = code_of(
        lambda x, a: x[a : a + 1, :], dot_nt(marks, volume_hot16), iota((1, volumes), 1)
    )
    code_col = code_of(
        lambda x, a: x[:, a : a + 1], dot_nt(volume_hot16, marks), iota((volumes, 1), 0)
    )
    same = iota((volumes, volumes), 0) // VOL_GRP == iota((volumes, volumes), 1) // VOL_GRP
    below = jnp.where(jnp.logical_and(same, code_row < code_col), 1, 0)
    rank_col = jnp.sum(below, axis=1, keepdims=True) + 1
    size = jnp.sum(jnp.where(volume_hot, rank_col, 0), axis=0, keepdims=True)
    key = (offset * NBMAX + size - 1) * rounds + turn
    key_hot = iota((UNIT * NBMAX * rounds, elems), 0) == key
    earlier = jnp.where(iota((elems, elems), 0) < iota((elems, elems), 1), 1.0, 0.0).astype(BF16)
    counts = dot_nn(jnp.where(key_hot, 1.0, 0.0).astype(BF16), earlier)
    rank = jnp.sum(jnp.where(key_hot, counts, 0.0), axis=0, keepdims=True).astype(I32)
    slot = offset * TILE + turn * (TILE // rounds) + rank
    place_out[...] = jnp.concatenate([slot, size, jnp.zeros((6, elems), I32)], axis=0)

    nodes = disp.shape[1]
    onehots = [node_onehot(conn[a : a + 1, :], nodes) for a in range(4)]
    found = gather_nodes(nodal_parts(disp[...]), onehots)
    strain = strain_rows(grads[...], found)
    strain8 = jnp.concatenate(strain + [volume.astype(F32), jnp.zeros((1, elems), F32)], axis=0)
    strain_out[...] = strain8
    first = jnp.concatenate([strain8, jnp.zeros((120, elems), F32)], axis=0).astype(BF16)
    second = jnp.concatenate(
        [jnp.zeros((64, elems), F32), strain8, jnp.zeros((56, elems), F32)], axis=0
    ).astype(BF16)
    hots = [class_onehot(slot, size, c + 1) for c in range(NBMAX)]
    for one, other, row0 in ((3, 0, 0), (2, 1, TILE)):
        extras = (dot_nt(hots[one], first) + dot_nt(hots[other], second)).astype(BF16)
        for k in range(UNIT):
            out[ids[5] ^ k, row0 : row0 + TILE, STATE_LANES:] = extras[TILE * k : TILE * (k + 1)]
    order = lane_order()
    for c in range(NBMAX):
        lane0, row0 = CLASS_PLACE[c]
        for a in range(c + 1):
            rows = dot_nn(hots[c], state_vmem[:, LEVEL * a : LEVEL * (a + 1)]).astype(BF16)
            rows = dot_nn(rows, order).astype(BF16)
            for k in range(UNIT):
                out[ids[5] ^ k, row0 : row0 + TILE, lane0 + LEVEL * a : lane0 + LEVEL * (a + 1)] = rows[
                    TILE * k : TILE * (k + 1)
                ]


def transpose_kernel(off, turned):
    for n in range(OFF_GRP):
        turned[n] = jnp.transpose(off[n])


def solve_kernel(ids, ints, small, blocks, off, msgs, *refs):
    outs, refs = refs[:UNIT], refs[UNIT:]
    tangents, state, low, rest, contact_scale, inverse, response, diag_pairs, off_pairs = refs
    extras = []
    for rank in range(NBMAX):
        row0 = CLASS_PLACE[rank][1]
        tile = jnp.concatenate([msgs[ids[5] ^ k, row0 : row0 + TILE, STATE_LANES:] for k in range(UNIT)], axis=0).astype(F32)
        extras.append(tile if rank >= 2 else pltpu.roll(tile, 64, 1))
    held = [[extras[rank][:, RANK_LANE : RANK_LANE + 1] == ints[6, c].astype(F32) for rank in range(NBMAX)] for c in range(NBMAX)]
    agree = functools.reduce(jnp.logical_and, [held[c][c] for c in range(NBMAX)])
    in_order = jnp.min(jnp.where(agree, 1.0, 0.0)) > 0.5

    @pl.when(in_order)
    def _():
        for c in range(NBMAX):
            lane0, row0 = CLASS_PLACE[c]
            for a in range(c + 1):
                r = CLASS_BASE[c] + a
                for j in range(COMPS):
                    lane = lane0 + LEVEL * a + BS * j
                    for k in range(UNIT):
                        piece = msgs[ids[5] ^ k, row0 : row0 + TILE, lane : lane + BS]
                        dst = slice(SLOTS * j + TILE * k, SLOTS * j + TILE * (k + 1))
                        low[r, dst, :] = piece
                        state[r, dst, :] = piece.astype(F32)

    @pl.when(jnp.logical_not(in_order))
    def _():
        def component(j, carry):
            for c in range(NBMAX):
                for a in range(c + 1):
                    r = CLASS_BASE[c] + a
                    total = jnp.zeros((SLOTS, BS), F32)
                    for rank in range(a, NBMAX):
                        lane0, row0 = CLASS_PLACE[rank]
                        lane = pl.multiple_of(lane0 + LEVEL * a + BS * j, BS)
                        piece = jnp.concatenate(
                            [msgs[ids[5] ^ k, row0 : row0 + TILE, pl.ds(lane, BS)] for k in range(UNIT)], axis=0
                        )
                        total = jnp.where(held[c][rank], piece.astype(F32), total)
                    dst = pl.ds(pl.multiple_of(SLOTS * j, SLOTS), SLOTS)
                    low[r, dst, :] = total.astype(BF16)
                    state[r, dst, :] = total
            return carry

        lax.fori_loop(0, COMPS, component, 0)

    normals = small[SM_NORMAL : SM_NORMAL + 8, :]
    normals = jnp.concatenate([normals, jnp.zeros((BS - 8, BS), F32)], axis=0)
    parts = split3(normals)
    for c in range(NBMAX):
        strains = jnp.zeros((SLOTS, BS), F32)
        for rank in range(NBMAX):
            strains = jnp.where(held[c][rank], extras[rank], strains)
        strains = strains.astype(BF16)
        dots = dot_nn(strains, parts[0]) + dot_nn(strains, parts[1]) + dot_nn(strains, parts[2])
        response[c] = 1.0 + GAIN_NORMAL * jnp.tanh(dots)
    eye = iota((BS, BS), 0) == iota((BS, BS), 1)
    diag_inverse = []
    for c in range(NBMAX):
        for a in range(c + 1):
            r = CLASS_BASE[c] + a
            values = jnp.sum(jnp.where(eye, blocks[r].astype(F32), 0.0), axis=0, keepdims=True)
            diag_inverse.append(1.0 / values)
            inverse[r] = jnp.broadcast_to(1.0 / response[c, :, r : r + 1], (SLOTS, BS)) * diag_inverse[r]
    for n in range(OFF_GRP):
        contact_scale[n] = (
            jnp.broadcast_to(response[ints[5, n], :, HALF_OFF + n : HALF_OFF + n + 1], (SLOTS, BS))
            * inverse[ints[4, n]]
        )
    zero = jnp.zeros((BS, BS), BF16)
    for p in range(HALF_ROWS // 2):
        diag_pairs[p, :BS, :BS] = blocks[2 * p]
        diag_pairs[p, :BS, BS:] = zero
        diag_pairs[p, BS:, :BS] = zero
        diag_pairs[p, BS:, BS:] = blocks[2 * p + 1]
    live = ints[0, 0]
    turns = (live + WIDE - 1) // WIDE

    def contact_block(m):
        n = ints[1, jnp.minimum(m, live - 1)]
        found = off[n]
        return jnp.where(m < live, found, zero)

    def fill(p, carry):
        off_pairs[p, :BS, :BS] = contact_block(2 * p)
        off_pairs[p, :BS, BS:] = zero
        off_pairs[p, BS:, :BS] = zero
        off_pairs[p, BS:, BS:] = contact_block(2 * p + 1)
        return carry

    lax.fori_loop(0, turns * (WIDE // 2), fill, 0)

    def contacts(t, carry):
        slots = [jnp.minimum(WIDE * t + i, live - 1) for i in range(WIDE)]
        cols = [ints[3, m] for m in slots]
        rows = [ints[2, m] for m in slots]
        which = [ints[1, m] for m in slots]
        for base in range(0, COMPS * SLOTS, CHUNK):
            span = slice(base, base + CHUNK)
            products = []
            for h in range(WIDE // 2):
                both = jnp.concatenate([low[cols[2 * h], span, :], low[cols[2 * h + 1], span, :]], axis=1)
                products.append(dot_nn(both, off_pairs[(WIDE // 2) * t + h]))
            for i in range(WIDE):
                scale = contact_scale[which[i]]
                for j in range(CHUNK // SLOTS):
                    part = products[i // 2][SLOTS * j : SLOTS * (j + 1), BS * (i % 2) : BS * (i % 2 + 1)]
                    state[rows[i], base + SLOTS * j : base + SLOTS * (j + 1), :] -= part * scale
        return carry

    def sweep(last):
        lax.fori_loop(0, turns, contacts, 0)
        for p in range(HALF_ROWS // 2):
            for base in range(0, COMPS * SLOTS, CHUNK):
                span = slice(base, base + CHUNK)
                both = jnp.concatenate([low[2 * p, span, :], low[2 * p + 1, span, :]], axis=1)
                product = dot_nt(both, diag_pairs[p])
                for i in range(2):
                    r = 2 * p + i
                    for j in range(CHUNK // SLOTS):
                        comp = base // SLOTS + j
                        at = slice(SLOTS * comp, SLOTS * (comp + 1))
                        part = product[SLOTS * j : SLOTS * (j + 1), BS * i : BS * (i + 1)]
                        load = small[8 * r + comp : 8 * r + comp + 1, :]
                        value = state[r, at, :] + (load * inverse[r] - part * diag_inverse[r])
                        high = value.astype(BF16)
                        low[r, at, :] = high
                        if last:
                            rest[r, at, :] = (value - high.astype(F32)).astype(BF16)
                        else:
                            state[r, at, :] = value

    lax.fori_loop(0, SWEEPS - 1, lambda step, carry: (sweep(False), carry)[1], 0)
    sweep(True)
    lane = iota((1, BS), 1)
    entries = []
    for c in range(NBMAX):
        weights, values = [], []
        for a in range(c + 1):
            r = CLASS_BASE[c] + a
            load8 = small[8 * r : 8 * r + 8, :]
            high = load8.astype(BF16).astype(F32)
            gap = jnp.zeros((16, BS), F32)
            both = jnp.concatenate([high] * 6 + [gap] + [load8 - high] * 6 + [gap], axis=0).astype(BF16)
            weights += [both, both]
            values += [low[r], rest[r]]
        product = dot_nt(jnp.concatenate(values, axis=1), jnp.concatenate(weights, axis=1))
        total = jnp.zeros((SLOTS, BS), F32)
        for j in range(COMPS):
            total = jnp.where((lane // 8) % 8 == j, product[SLOTS * j : SLOTS * (j + 1)], total)
        total = total + pltpu.roll(total, 64, 1)
        found = sum(jnp.where(held[c][rank], rank + 1.0, 0.0) for rank in range(NBMAX))
        entry = small[SM_AFFINE + c : SM_AFFINE + c + 1, :] - total / ((c + 1) * BS)
        entries.append(jnp.where(lane % 64 == RANK_LANE, found, entry))
    for row0, one, two in ((0, 3, 0), (TILE, 2, 1)):
        packed = jnp.where(lane < 64, entries[one], entries[two]).astype(BF16)
        for k in range(UNIT):
            tangents[ids[5] ^ k, row0 : row0 + TILE, :] = packed[TILE * k : TILE * (k + 1)]
    for c in range(NBMAX):
        lane0, row0 = CLASS_PLACE[c]
        for a in range(c + 1):
            r = CLASS_BASE[c] + a
            for j in range(COMPS):
                lane_at = lane0 + LEVEL * a + BS * j
                for k in range(UNIT):
                    outs[k][row0 : row0 + TILE, lane_at : lane_at + BS] = low[
                        r, SLOTS * j + TILE * k : SLOTS * j + TILE * (k + 1), :
                    ]


def fem_kernel(ids, tangents, place, strain, grads, volume, conn, nodal_load, residual, product, norm):
    elems = place.shape[1]
    nodes = nodal_load.shape[1]
    slot, size = place[0:1, :], place[1:2, :]
    packed, hots = returned_onehots(ids, tangents, slot, size)
    entries = jnp.zeros((64, elems), F32)
    for tile, one, two in ((packed[0], 3, 0), (packed[1], 2, 1)):
        entries += dot_tn(tile, hots[one])[:64]
        entries += dot_tn(tile, hots[two])[64:]
    entry = lambda i, j: entries[8 * j + i : 8 * j + i + 1]
    weight = volume[...]
    g_all = grads[...]
    g = lambda a, k: g_all[3 * a + k : 3 * a + k + 1]
    onehots = [node_onehot(conn[a : a + 1, :], nodes) for a in range(4)]

    def assemble(strains):
        s = []
        for i in range(COMPS):
            total = entry(i, 0) * strains[0]
            for j in range(1, COMPS):
                total = total + entry(i, j) * strains[j]
            s.append(total * weight)
        result = jnp.zeros((TILE, nodes), F32)
        for a in range(4):
            force = jnp.concatenate(
                [
                    g(a, 0) * s[0] + g(a, 2) * s[4] + g(a, 1) * s[5],
                    g(a, 1) * s[1] + g(a, 2) * s[3] + g(a, 0) * s[5],
                    g(a, 2) * s[2] + g(a, 1) * s[3] + g(a, 0) * s[4],
                ],
                axis=0,
            )
            result += dot_nt(nodal_parts(force), onehots[a])
        return result[0:3] + result[3:6] + result[6:9]

    strains = strain[...]
    res = assemble([strains[i : i + 1] for i in range(COMPS)]) - nodal_load[...]
    residual[...] = res
    norm[...] = jnp.broadcast_to(jnp.sum(res * res, keepdims=True), norm.shape)
    trial = strain_rows(g_all, gather_nodes(nodal_parts(res), onehots))
    product[...] = assemble(trial)


def unpack_kernel(ids, place, tangents, *refs):
    msgs, (out, out_vmem, sems) = refs[:UNIT], refs[UNIT:]
    slot, size = place[0:1, :], place[1:2, :]
    order = lane_order_back()
    hots = [jnp.transpose(hot) for hot in returned_onehots(ids, tangents, slot, size)[1]]
    copies = []
    for a in range(NBMAX):
        pieces = []
        for c in range(a, NBMAX):
            lane0, row0 = CLASS_PLACE[c]
            lane = lane0 + LEVEL * a
            rows = jnp.concatenate([msgs[k][row0 : row0 + TILE, lane : lane + LEVEL] for k in range(UNIT)], axis=0)
            pieces.append(dot_nn(rows, order).astype(BF16))
        hot = jnp.concatenate(hots[a:], axis=1)
        out_vmem[a] = dot_nn(hot, jnp.concatenate(pieces, axis=0)).astype(BF16)
        copy = pltpu.make_async_copy(out_vmem.at[a], out.at[:, pl.ds(LEVEL * a, LEVEL)], sems.at[a])
        copy.start()
        copies.append(copy)
    for copy in copies:
        copy.wait()


def spec(space):
    return pl.BlockSpec(memory_space=space)


VM, SM, HB = pltpu.VMEM, pltpu.SMEM, pl.ANY


def call(kernel, args, spaces, outs, out_spaces, scratch, cost=None):
    return pl.pallas_call(
        kernel,
        out_shape=[jax.ShapeDtypeStruct(s, d) for s, d in outs],
        in_specs=[spec(s) for s in spaces],
        out_specs=[spec(s) for s in out_spaces],
        scratch_shapes=scratch,
        compiler_params=pltpu.CompilerParams(vmem_limit_bytes=VMEM_LIMIT),
        cost_estimate=cost,
    )(*args)


def solve_call(*args):
    return call(
        solve_kernel,
        args,
        (SM, SM) + (VM,) * 4,
        tuple(((2 * TILE, STATE_LANES), BF16) for _ in range(UNIT)) + (((UNIT, 2 * TILE, BS), BF16),),
        (VM,) * (UNIT + 1),
        [
            pltpu.VMEM((HALF_ROWS, COMPS * SLOTS, BS), F32),
            pltpu.VMEM((HALF_ROWS, COMPS * SLOTS, BS), BF16),
            pltpu.VMEM((HALF_ROWS, COMPS * SLOTS, BS), BF16),
            pltpu.VMEM((OFF_GRP, SLOTS, BS), F32),
            pltpu.VMEM((HALF_ROWS, SLOTS, BS), F32),
            pltpu.VMEM((NBMAX, SLOTS, BS), F32),
            pltpu.VMEM((HALF_ROWS // 2, 2 * BS, 2 * BS), BF16),
            pltpu.VMEM((OFF_GRP // 2, 2 * BS, 2 * BS), BF16),
        ],
    )


def pack_call(groups, rounds, *args):
    elems = args[1].shape[1]
    return call(
        functools.partial(pack_kernel, groups, rounds),
        args,
        (SM, VM, VM, VM, VM, HB),
        (((UNIT, 2 * TILE, MSG_LANES), BF16), ((8, elems), F32), ((8, elems), I32)),
        (VM,) * 3,
        [pltpu.VMEM((elems, NBMAX * LEVEL), BF16), pltpu.SemaphoreType.DMA],
    )


def unpack_call(*args):
    elems = args[1].shape[1]
    return call(
        unpack_kernel,
        args,
        (SM,) + (VM,) * (UNIT + 2),
        (((elems, NBMAX * LEVEL), BF16),),
        (HB,),
        [pltpu.VMEM((NBMAX, elems, LEVEL), BF16), pltpu.SemaphoreType.DMA((NBMAX,))],
    )


def on_device(
    shape,
    displacement, nodal_load, connectivity, shape_grads, elem_volume, point_map, vol_blocks, c_affine,
    coupling, diag_blocks, diag_normal, off_blocks, off_row, off_col, off_normal, off_count, fluct_state,
):
    z_count = shape[2]
    groups = z_count * 4
    rounds = z_count // 2
    devices = 4 * groups
    elems = connectivity.shape[1]
    node_count = displacement.shape[1]
    index = {name: lax.axis_index(name) for name in AXES}
    unit_index = index["x"] * 4 + index["l"] * 2 + index["c"]
    ids = jnp.stack(
        [index["y"], index["x"], index["h"], index["l"], index["c"], unit_index, unit_index, unit_index]
    ).astype(I32)

    def coords(device):
        section, group = divmod(device, groups)
        return section // 2, section % 2, group // 4, (group // 2) % 2, group % 2

    def number(y, x, h, l, c):
        return (y * 2 + x) * groups + h * 4 + l * 2 + c

    def permute(value, source_of):
        pairs = [(number(*source_of(*coords(d))), d) for d in range(devices)]
        return lax.ppermute(value, AXES, pairs)

    def unit_permute(value, k):
        return permute(value, lambda y, x, h, l, c: (y, x ^ (k >> 2), h, l ^ ((k >> 1) & 1), c ^ (k & 1)))

    def normal_rows(normals):
        return jnp.pad(normals.transpose(2, 1, 0)[:, 0], ((0, 2), (0, BS - normals.shape[0])))

    diag_half, small, ints = call(
        matrix_pack_kernel,
        (
            ids, vol_blocks, off_row.T, off_col.T, off_count, coupling.reshape(ROWS_GRP * COMPS, BS),
            normal_rows(diag_normal), normal_rows(off_normal), c_affine[0], diag_blocks[:, 0],
        ),
        (SM, SM, SM, SM, SM, VM, VM, VM, VM, HB),
        (((HALF_ROWS, BS, BS), BF16), ((SM_ROWS, BS), F32), ((8, BS), I32)),
        (VM, VM, SM),
        [
            pltpu.SMEM((32,), I32), pltpu.SMEM((32,), I32), pltpu.SMEM((16,), I32), pltpu.SMEM((8,), I32),
            pltpu.SemaphoreType.DMA((HALF_ROWS,)),
        ],
    )
    packed, strain, place = pack_call(
        groups, rounds, ids, point_map.reshape(1, elems), displacement, connectivity, shape_grads, fluct_state
    )
    msgs = lax.all_to_all(packed, UNIT_AXES, split_axis=0, concat_axis=0, tiled=True)

    solved = None
    for turn in range(rounds):
        def from_group(y, x, h, l, c, turn=turn):
            return y, x, (h + 2 * turn + (x ^ c)) % z_count, l, c

        off_t, diag_t, small_t, ints_t = [
            permute(value, from_group) for value in (off_blocks[:, 0], diag_half, small, ints)
        ]
        (off_t,) = call(
            transpose_kernel,
            (off_t,),
            (VM,),
            (((OFF_GRP, BS, BS), BF16),),
            (VM,),
            [],
            pl.CostEstimate(flops=60_000_000_000, bytes_accessed=200_000_000, transcendentals=0),
        )
        result = solve_call(ids, ints_t, small_t, diag_t, off_t, msgs)
        if solved is None:
            solved = result
        else:
            of_turn = (jnp.arange(2 * TILE) % TILE) // (TILE // rounds) == turn
            solved = [jnp.where(of_turn[:, None], new, old) for new, old in zip(result, solved)]

    back = [solved[0]] + [unit_permute(solved[k], k) for k in range(1, UNIT)]
    own, back[4] = lax.optimization_barrier((solved[UNIT], back[4]))
    tangents = lax.all_to_all(own, UNIT_AXES, split_axis=0, concat_axis=0, tiled=True)
    residual, product, norm = call(
        fem_kernel,
        (ids, tangents, place, strain, shape_grads, elem_volume.reshape(1, elems), connectivity, nodal_load),
        (SM,) + (VM,) * 7,
        (((3, node_count), F32), ((3, node_count), F32), ((devices, BS), F32)),
        (VM,) * 3,
        [],
    )
    norms = lax.all_to_all(norm, AXES, split_axis=0, concat_axis=0, tiled=True)
    norm_sq = jnp.sum(norms[:, 0])
    root_mean = jnp.sqrt(norm_sq / (3.0 * node_count * devices) + 1e-06)
    update = -jnp.minimum(1.0, CLIP_RMS / root_mean) * residual
    (fluct_new,) = unpack_call(ids, place, tangents, *back)
    return residual, product, update, fluct_new


def solution(mesh):
    sections, groups = mesh.shape["sec"], mesh.shape["bulk"]
    shape = (2, sections // 2, groups // 4, 2, 2)
    fine = Mesh(mesh.devices.reshape(shape), AXES)
    return jax.shard_map(
        functools.partial(on_device, shape),
        mesh=fine,
        in_specs=(
            P(None, AXES),
            P(None, AXES),
            P(None, AXES),
            P(None, AXES),
            P(AXES),
            P(AXES),
            P(GROUP_AXES, None),
            P(GROUP_AXES, None, None),
            P(None, GROUP_AXES, None, None),
            P(None, GROUP_AXES, None, None),
            P(None, GROUP_AXES, None),
            P(None, GROUP_AXES, None, None),
            P(None, GROUP_AXES),
            P(None, GROUP_AXES),
            P(None, GROUP_AXES, None),
            P(GROUP_AXES),
            P(AXES, None),
        ),
        out_specs=(P(None, AXES), P(None, AXES), P(None, AXES), P(AXES, None)),
        check_vma=False,
    )
```

```python
import functools

import jax
import jax.numpy as jnp
from jax import lax
from jax.experimental import pallas as pl
from jax.experimental.pallas import tpu as pltpu
from jax.sharding import Mesh, PartitionSpec as P

BS = 128
NBMAX = 4
VOL_GRP = 8
GPV_DEV = 64
SWEEPS = 3
ROWS_GRP = 20
HALF_ROWS = 10
OFF_GRP = 32
HALF_OFF = 16
COMPS = 6
LEVEL = BS * COMPS
UNIT = 8
TILE = 16
SLOTS = UNIT * TILE
STATE_LANES = 5 * LEVEL
MSG_LANES = STATE_LANES + 128
GAIN_NORMAL = 0.4
WIDE = 8
CHUNK = 256
CLIP_RMS = 1.0
SM_NORMAL = 80
SM_AFFINE = 88
SM_ROWS = 96
RANK_LANE = 6

F32 = jnp.float32
BF16 = jnp.bfloat16
I32 = jnp.int32
AXES = ("y", "x", "h", "l", "c")
GROUP_AXES = ("h", "l", "c")
UNIT_AXES = ("x", "l", "c")
VMEM_LIMIT = 56 * 1024 * 1024

CLASS_PLACE = ((4 * LEVEL, 0), (3 * LEVEL, TILE), (0, TILE), (0, 0))
CLASS_BASE = (0, 1, 3, 6)


def dot_nn(lhs, rhs):
    return lax.dot_general(lhs, rhs, (((1,), (0,)), ((), ())), preferred_element_type=F32)


def dot_nt(lhs, rhs):
    return lax.dot_general(lhs, rhs, (((1,), (1,)), ((), ())), preferred_element_type=F32)


def dot_tn(lhs, rhs):
    return lax.dot_general(lhs, rhs, (((0,), (0,)), ((), ())), preferred_element_type=F32)


def split3(value):
    high = value.astype(BF16)
    rest = value - high.astype(F32)
    mid = rest.astype(BF16)
    low = (rest - mid.astype(F32)).astype(BF16)
    return high, mid, low


def iota(shape, dim):
    return lax.broadcasted_iota(I32, shape, dim)


def lane_order():
    target = iota((1, LEVEL), 1)
    source = COMPS * (target % BS) + target // BS
    return jnp.where(iota((LEVEL, LEVEL), 0) == source, 1.0, 0.0).astype(BF16)


def lane_order_back():
    row = iota((LEVEL, 1), 0)
    return jnp.where(iota((LEVEL, LEVEL), 1) == COMPS * (row % BS) + row // BS, 1.0, 0.0).astype(BF16)


def class_onehot(slot, size, level_rows):
    chosen = jnp.where(size == level_rows, slot, -1)
    return jnp.where(iota((SLOTS, slot.shape[1]), 0) == chosen, 1.0, 0.0).astype(BF16)


def returned_onehots(ids, tangents, slot, rank):
    packed, hots = [], [None] * NBMAX
    wanted = rank * SLOTS + slot
    place = iota((SLOTS, 1), 0)
    for row0, one, two in ((0, 3, 0), (TILE, 2, 1)):
        tile = jnp.concatenate([tangents[ids[5] ^ k, row0 : row0 + TILE, :] for k in range(UNIT)], axis=0)
        packed.append(tile)
        for c, lane in ((one, RANK_LANE), (two, 64 + RANK_LANE)):
            at = tile[:, lane : lane + 1].astype(F32).astype(I32) * SLOTS + place
            hots[c] = jnp.where(wanted == at, 1.0, 0.0).astype(BF16)
    return packed, hots


def node_onehot(conn_row, nodes):
    return jnp.where(iota((nodes, conn_row.shape[1]), 0) == conn_row, 1.0, 0.0).astype(BF16)


def nodal_parts(nodal):
    parts = [jnp.concatenate([p.astype(F32), jnp.zeros((13, p.shape[1]), F32)], axis=0) for p in split3(nodal)]
    rows = parts[0] + pltpu.roll(parts[1], 3, 0) + pltpu.roll(parts[2], 6, 0)
    return rows.astype(BF16)


def gather_nodes(rows, onehots):
    found = []
    for onehot in onehots:
        got = dot_nn(rows, onehot)
        found.append([got[i : i + 1] + got[i + 3 : i + 4] + got[i + 6 : i + 7] for i in range(3)])
    return found


def strain_rows(grads, disp):
    g = lambda a, k: grads[3 * a + k : 3 * a + k + 1]
    total = lambda f: f(0) + f(1) + f(2) + f(3)
    return [
        total(lambda a: g(a, 0) * disp[a][0]),
        total(lambda a: g(a, 1) * disp[a][1]),
        total(lambda a: g(a, 2) * disp[a][2]),
        total(lambda a: g(a, 2) * disp[a][1] + g(a, 1) * disp[a][2]),
        total(lambda a: g(a, 2) * disp[a][0] + g(a, 0) * disp[a][2]),
        total(lambda a: g(a, 1) * disp[a][0] + g(a, 0) * disp[a][1]),
    ]


def matrix_pack_kernel(
    ids, vol, off_row, off_col, off_count, coupling, diag_normal, off_normal, affine, diag,
    diag_out, small, ints, row_local, row_size, rows_sel, seen, loads, sems,
):
    half = ids[0]
    small[...] = jnp.zeros_like(small)
    loads[...] = jnp.zeros_like(loads)
    loads[0 : ROWS_GRP * COMPS, :] = coupling[...]
    small[0:VOL_GRP, 0:36] = affine[...]
    target = iota((1, BS), 1) % 64
    source = jnp.where(jnp.logical_and(target % 8 < 6, target < 48), 6 * (target % 8) + target // 8, -1)
    shift = jnp.where(iota((BS, BS), 0) == source, 1.0, 0.0).astype(BF16)
    moved = sum(dot_nn(part, shift) for part in split3(small[0:VOL_GRP, :]))
    small[0:VOL_GRP, :] = jnp.zeros((VOL_GRP, BS), F32)
    for size in range(NBMAX + 1):
        seen[size] = 0
    start = 0
    for v in range(VOL_GRP):
        size = vol[0, v]
        rank = seen[size]
        seen[size] = rank + 1
        mine = rank == half
        base = (size * (size - 1)) // 2
        for a in range(NBMAX):
            @pl.when(a < size)
            def _(a=a, size=size, base=base, mine=mine, start=start):
                row_local[start + a] = jnp.where(mine, base + a, -1)
                row_size[start + a] = size - 1

            @pl.when(jnp.logical_and(a < size, mine))
            def _(a=a, base=base, start=start):
                rows_sel[base + a] = start + a

        @pl.when(mine)
        def _(size=size, v=v):
            small[pl.ds(SM_AFFINE - 1 + size, 1), :] = moved[v : v + 1, :]
            ints[6, size - 1] = v

        start = start + size
    copies = []
    for i in range(HALF_ROWS):
        copies.append(
            pltpu.make_async_copy(diag.at[pl.ds(rows_sel[i], 1)], diag_out.at[pl.ds(i, 1)], sems.at[i])
        )
        copies[-1].start()
    lane = iota((8, BS), 1)
    normals = jnp.zeros((8, BS), F32)
    diag_rows = diag_normal[...]
    for i in range(HALF_ROWS):
        row = rows_sel[i]
        small[8 * i : 8 * i + COMPS, :] = loads[pl.ds(COMPS * row, COMPS), :]
        normals += jnp.where(lane == i, pltpu.roll(diag_rows, (i - row + BS) % BS, 1), 0.0)
    normals += pltpu.roll(off_normal[...], HALF_OFF, 1)
    small[SM_NORMAL : SM_NORMAL + 8, :] = normals
    live_total = off_count[0]

    def contact(n, found):
        row = off_row[0, n]
        local = row_local[row]
        ints[4, n] = jnp.maximum(local, 0)
        ints[5, n] = row_size[row]
        live = jnp.logical_and(n < live_total, local >= 0)

        @pl.when(live)
        def _():
            ints[1, found] = n
            ints[2, found] = local
            ints[3, found] = row_local[off_col[0, n]]

        return found + live.astype(I32)

    ints[0, 0] = lax.fori_loop(0, OFF_GRP, contact, 0)
    for copy in copies:
        copy.wait()


def pack_kernel(groups, rounds, ids, point_map, disp, conn, grads, state, *refs):
    out, strain_out, place_out, state_vmem, sem = refs
    load = pltpu.make_async_copy(state, state_vmem, sem)
    load.start()
    elems = point_map.shape[1]
    x_me, h_me, l_me, c_me = ids[1], ids[2], ids[3], ids[4]
    z_count = groups // 4
    codes = point_map[...]
    owner = codes // elems
    within = codes % elems
    group = owner % groups
    volume = within // GPV_DEV
    delta = (group // 4 - h_me + z_count) % z_count
    core = group % 2
    low = (group // 2) % 2
    across = (delta % 2) ^ core
    turn = delta // 2
    offset = ((across ^ x_me) * 4) + ((low ^ l_me) * 2) + (core ^ c_me)
    volumes = groups * VOL_GRP
    volume_hot = iota((volumes, elems), 0) == group * VOL_GRP + volume
    volume_hot16 = jnp.where(volume_hot, 1.0, 0.0).astype(BF16)
    load.wait()
    ones = jnp.ones((8, LEVEL), BF16)
    filled = jnp.concatenate(
        [dot_nt(ones, jnp.abs(state_vmem[:, LEVEL * a : LEVEL * (a + 1)]))[0:1] for a in range(NBMAX)], axis=0
    )
    marks = jnp.concatenate(
        [jnp.where(filled > 0.0, 1.0, 0.0), jnp.ones((1, elems), F32), jnp.zeros((3, elems), F32)], axis=0
    ).astype(BF16)

    def code_of(take, counts, number):
        height = jnp.zeros_like(number)
        for a in range(NBMAX):
            height = jnp.where(take(counts, a) > 0.0, a + 1, height)
        return jnp.where(take(counts, NBMAX) > 0.0, height * VOL_GRP + number % VOL_GRP, 1 << 20)

    code_row = code_of(
        lambda x, a: x[a : a + 1, :], dot_nt(marks, volume_hot16), iota((1, volumes), 1)
    )
    code_col = code_of(
        lambda x, a: x[:, a : a + 1], dot_nt(volume_hot16, marks), iota((volumes, 1), 0)
    )
    same = iota((volumes, volumes), 0) // VOL_GRP == iota((volumes, volumes), 1) // VOL_GRP
    below = jnp.where(jnp.logical_and(same, code_row < code_col), 1, 0)
    rank_col = jnp.sum(below, axis=1, keepdims=True) + 1
    size = jnp.sum(jnp.where(volume_hot, rank_col, 0), axis=0, keepdims=True)
    key = (offset * NBMAX + size - 1) * rounds + turn
    key_hot = iota((UNIT * NBMAX * rounds, elems), 0) == key
    earlier = jnp.where(iota((elems, elems), 0) < iota((elems, elems), 1), 1.0, 0.0).astype(BF16)
    counts = dot_nn(jnp.where(key_hot, 1.0, 0.0).astype(BF16), earlier)
    rank = jnp.sum(jnp.where(key_hot, counts, 0.0), axis=0, keepdims=True).astype(I32)
    slot = offset * TILE + turn * (TILE // rounds) + rank
    place_out[...] = jnp.concatenate([slot, size, jnp.zeros((6, elems), I32)], axis=0)

    nodes = disp.shape[1]
    onehots = [node_onehot(conn[a : a + 1, :], nodes) for a in range(4)]
    found = gather_nodes(nodal_parts(disp[...]), onehots)
    strain = strain_rows(grads[...], found)
    strain8 = jnp.concatenate(strain + [volume.astype(F32), jnp.zeros((1, elems), F32)], axis=0)
    strain_out[...] = strain8
    first = jnp.concatenate([strain8, jnp.zeros((120, elems), F32)], axis=0).astype(BF16)
    second = jnp.concatenate(
        [jnp.zeros((64, elems), F32), strain8, jnp.zeros((56, elems), F32)], axis=0
    ).astype(BF16)
    hots = [class_onehot(slot, size, c + 1) for c in range(NBMAX)]
    for one, other, row0 in ((3, 0, 0), (2, 1, TILE)):
        extras = (dot_nt(hots[one], first) + dot_nt(hots[other], second)).astype(BF16)
        for k in range(UNIT):
            out[ids[5] ^ k, row0 : row0 + TILE, STATE_LANES:] = extras[TILE * k : TILE * (k + 1)]
    order = lane_order()
    for c in range(NBMAX):
        lane0, row0 = CLASS_PLACE[c]
        for a in range(c + 1):
            rows = dot_nn(hots[c], state_vmem[:, LEVEL * a : LEVEL * (a + 1)]).astype(BF16)
            rows = dot_nn(rows, order).astype(BF16)
            for k in range(UNIT):
                out[ids[5] ^ k, row0 : row0 + TILE, lane0 + LEVEL * a : lane0 + LEVEL * (a + 1)] = rows[
                    TILE * k : TILE * (k + 1)
                ]


def transpose_kernel(off, turned):
    for n in range(OFF_GRP):
        turned[n] = jnp.transpose(off[n])


def solve_kernel(ids, ints, small, blocks, off, msgs, *refs):
    outs, refs = refs[:UNIT], refs[UNIT:]
    tangents, state, low, rest, contact_scale, inverse, response, diag_pairs, off_pairs = refs
    extras = []
    for rank in range(NBMAX):
        row0 = CLASS_PLACE[rank][1]
        tile = jnp.concatenate([msgs[ids[5] ^ k, row0 : row0 + TILE, STATE_LANES:] for k in range(UNIT)], axis=0).astype(F32)
        extras.append(tile if rank >= 2 else pltpu.roll(tile, 64, 1))
    held = [[extras[rank][:, RANK_LANE : RANK_LANE + 1] == ints[6, c].astype(F32) for rank in range(NBMAX)] for c in range(NBMAX)]
    agree = functools.reduce(jnp.logical_and, [held[c][c] for c in range(NBMAX)])
    in_order = jnp.min(jnp.where(agree, 1.0, 0.0)) > 0.5

    @pl.when(in_order)
    def _():
        for c in range(NBMAX):
            lane0, row0 = CLASS_PLACE[c]
            for a in range(c + 1):
                r = CLASS_BASE[c] + a
                for j in range(COMPS):
                    lane = lane0 + LEVEL * a + BS * j
                    for k in range(UNIT):
                        piece = msgs[ids[5] ^ k, row0 : row0 + TILE, lane : lane + BS]
                        dst = slice(SLOTS * j + TILE * k, SLOTS * j + TILE * (k + 1))
                        low[r, dst, :] = piece
                        state[r, dst, :] = piece.astype(F32)

    @pl.when(jnp.logical_not(in_order))
    def _():
        def component(j, carry):
            for c in range(NBMAX):
                for a in range(c + 1):
                    r = CLASS_BASE[c] + a
                    total = jnp.zeros((SLOTS, BS), F32)
                    for rank in range(a, NBMAX):
                        lane0, row0 = CLASS_PLACE[rank]
                        lane = pl.multiple_of(lane0 + LEVEL * a + BS * j, BS)
                        piece = jnp.concatenate(
                            [msgs[ids[5] ^ k, row0 : row0 + TILE, pl.ds(lane, BS)] for k in range(UNIT)], axis=0
                        )
                        total = jnp.where(held[c][rank], piece.astype(F32), total)
                    dst = pl.ds(pl.multiple_of(SLOTS * j, SLOTS), SLOTS)
                    low[r, dst, :] = total.astype(BF16)
                    state[r, dst, :] = total
            return carry

        lax.fori_loop(0, COMPS, component, 0)

    normals = small[SM_NORMAL : SM_NORMAL + 8, :]
    normals = jnp.concatenate([normals, jnp.zeros((BS - 8, BS), F32)], axis=0)
    parts = split3(normals)
    for c in range(NBMAX):
        strains = jnp.zeros((SLOTS, BS), F32)
        for rank in range(NBMAX):
            strains = jnp.where(held[c][rank], extras[rank], strains)
        strains = strains.astype(BF16)
        dots = dot_nn(strains, parts[0]) + dot_nn(strains, parts[1]) + dot_nn(strains, parts[2])
        response[c] = 1.0 + GAIN_NORMAL * jnp.tanh(dots)
    eye = iota((BS, BS), 0) == iota((BS, BS), 1)
    diag_inverse = []
    for c in range(NBMAX):
        for a in range(c + 1):
            r = CLASS_BASE[c] + a
            values = jnp.sum(jnp.where(eye, blocks[r].astype(F32), 0.0), axis=0, keepdims=True)
            diag_inverse.append(1.0 / values)
            inverse[r] = jnp.broadcast_to(1.0 / response[c, :, r : r + 1], (SLOTS, BS)) * diag_inverse[r]
    for n in range(OFF_GRP):
        contact_scale[n] = (
            jnp.broadcast_to(response[ints[5, n], :, HALF_OFF + n : HALF_OFF + n + 1], (SLOTS, BS))
            * inverse[ints[4, n]]
        )
    zero = jnp.zeros((BS, BS), BF16)
    for p in range(HALF_ROWS // 2):
        diag_pairs[p, :BS, :BS] = blocks[2 * p]
        diag_pairs[p, :BS, BS:] = zero
        diag_pairs[p, BS:, :BS] = zero
        diag_pairs[p, BS:, BS:] = blocks[2 * p + 1]
    live = ints[0, 0]
    turns = (live + WIDE - 1) // WIDE

    def contact_block(m):
        n = ints[1, jnp.minimum(m, live - 1)]
        found = off[n]
        return jnp.where(m < live, found, zero)

    def fill(p, carry):
        off_pairs[p, :BS, :BS] = contact_block(2 * p)
        off_pairs[p, :BS, BS:] = zero
        off_pairs[p, BS:, :BS] = zero
        off_pairs[p, BS:, BS:] = contact_block(2 * p + 1)
        return carry

    lax.fori_loop(0, turns * (WIDE // 2), fill, 0)

    def contacts(t, carry):
        slots = [jnp.minimum(WIDE * t + i, live - 1) for i in range(WIDE)]
        cols = [ints[3, m] for m in slots]
        rows = [ints[2, m] for m in slots]
        which = [ints[1, m] for m in slots]
        for base in range(0, COMPS * SLOTS, CHUNK):
            span = slice(base, base + CHUNK)
            products = []
            for h in range(WIDE // 2):
                both = jnp.concatenate([low[cols[2 * h], span, :], low[cols[2 * h + 1], span, :]], axis=1)
                products.append(dot_nn(both, off_pairs[(WIDE // 2) * t + h]))
            for i in range(WIDE):
                scale = contact_scale[which[i]]
                for j in range(CHUNK // SLOTS):
                    part = products[i // 2][SLOTS * j : SLOTS * (j + 1), BS * (i % 2) : BS * (i % 2 + 1)]
                    state[rows[i], base + SLOTS * j : base + SLOTS * (j + 1), :] -= part * scale
        return carry

    def sweep(last):
        lax.fori_loop(0, turns, contacts, 0)
        for p in range(HALF_ROWS // 2):
            for base in range(0, COMPS * SLOTS, CHUNK):
                span = slice(base, base + CHUNK)
                both = jnp.concatenate([low[2 * p, span, :], low[2 * p + 1, span, :]], axis=1)
                product = dot_nt(both, diag_pairs[p])
                for i in range(2):
                    r = 2 * p + i
                    for j in range(CHUNK // SLOTS):
                        comp = base // SLOTS + j
                        at = slice(SLOTS * comp, SLOTS * (comp + 1))
                        part = product[SLOTS * j : SLOTS * (j + 1), BS * i : BS * (i + 1)]
                        load = small[8 * r + comp : 8 * r + comp + 1, :]
                        value = state[r, at, :] + (load * inverse[r] - part * diag_inverse[r])
                        high = value.astype(BF16)
                        low[r, at, :] = high
                        if last:
                            rest[r, at, :] = (value - high.astype(F32)).astype(BF16)
                        else:
                            state[r, at, :] = value

    lax.fori_loop(0, SWEEPS - 1, lambda step, carry: (sweep(False), carry)[1], 0)
    sweep(True)
    lane = iota((1, BS), 1)
    entries = []
    for c in range(NBMAX):
        weights, values = [], []
        for a in range(c + 1):
            r = CLASS_BASE[c] + a
            load8 = small[8 * r : 8 * r + 8, :]
            high = load8.astype(BF16).astype(F32)
            gap = jnp.zeros((16, BS), F32)
            both = jnp.concatenate([high] * 6 + [gap] + [load8 - high] * 6 + [gap], axis=0).astype(BF16)
            weights += [both, both]
            values += [low[r], rest[r]]
        product = dot_nt(jnp.concatenate(values, axis=1), jnp.concatenate(weights, axis=1))
        total = jnp.zeros((SLOTS, BS), F32)
        for j in range(COMPS):
            total = jnp.where((lane // 8) % 8 == j, product[SLOTS * j : SLOTS * (j + 1)], total)
        total = total + pltpu.roll(total, 64, 1)
        found = sum(jnp.where(held[c][rank], rank + 1.0, 0.0) for rank in range(NBMAX))
        entry = small[SM_AFFINE + c : SM_AFFINE + c + 1, :] - total / ((c + 1) * BS)
        entries.append(jnp.where(lane % 64 == RANK_LANE, found, entry))
    for row0, one, two in ((0, 3, 0), (TILE, 2, 1)):
        packed = jnp.where(lane < 64, entries[one], entries[two]).astype(BF16)
        for k in range(UNIT):
            tangents[ids[5] ^ k, row0 : row0 + TILE, :] = packed[TILE * k : TILE * (k + 1)]
    for c in range(NBMAX):
        lane0, row0 = CLASS_PLACE[c]
        for a in range(c + 1):
            r = CLASS_BASE[c] + a
            for j in range(COMPS):
                lane_at = lane0 + LEVEL * a + BS * j
                for k in range(UNIT):
                    outs[k][row0 : row0 + TILE, lane_at : lane_at + BS] = low[
                        r, SLOTS * j + TILE * k : SLOTS * j + TILE * (k + 1), :
                    ]


def fem_kernel(ids, tangents, place, strain, grads, volume, conn, nodal_load, residual, product, norm):
    elems = place.shape[1]
    nodes = nodal_load.shape[1]
    slot, size = place[0:1, :], place[1:2, :]
    packed, hots = returned_onehots(ids, tangents, slot, size)
    entries = jnp.zeros((64, elems), F32)
    for tile, one, two in ((packed[0], 3, 0), (packed[1], 2, 1)):
        entries += dot_tn(tile, hots[one])[:64]
        entries += dot_tn(tile, hots[two])[64:]
    entry = lambda i, j: entries[8 * j + i : 8 * j + i + 1]
    weight = volume[...]
    g_all = grads[...]
    g = lambda a, k: g_all[3 * a + k : 3 * a + k + 1]
    onehots = [node_onehot(conn[a : a + 1, :], nodes) for a in range(4)]

    def assemble(strains):
        s = []
        for i in range(COMPS):
            total = entry(i, 0) * strains[0]
            for j in range(1, COMPS):
                total = total + entry(i, j) * strains[j]
            s.append(total * weight)
        result = jnp.zeros((TILE, nodes), F32)
        for a in range(4):
            force = jnp.concatenate(
                [
                    g(a, 0) * s[0] + g(a, 2) * s[4] + g(a, 1) * s[5],
                    g(a, 1) * s[1] + g(a, 2) * s[3] + g(a, 0) * s[5],
                    g(a, 2) * s[2] + g(a, 1) * s[3] + g(a, 0) * s[4],
                ],
                axis=0,
            )
            result += dot_nt(nodal_parts(force), onehots[a])
        return result[0:3] + result[3:6] + result[6:9]

    strains = strain[...]
    res = assemble([strains[i : i + 1] for i in range(COMPS)]) - nodal_load[...]
    residual[...] = res
    norm[...] = jnp.broadcast_to(jnp.sum(res * res, keepdims=True), norm.shape)
    trial = strain_rows(g_all, gather_nodes(nodal_parts(res), onehots))
    product[...] = assemble(trial)


def unpack_kernel(ids, place, tangents, *refs):
    msgs, (out, out_vmem, sems) = refs[:UNIT], refs[UNIT:]
    slot, size = place[0:1, :], place[1:2, :]
    order = lane_order_back()
    hots = [jnp.transpose(hot) for hot in returned_onehots(ids, tangents, slot, size)[1]]
    copies = []
    for a in range(NBMAX):
        pieces = []
        for c in range(a, NBMAX):
            lane0, row0 = CLASS_PLACE[c]
            lane = lane0 + LEVEL * a
            rows = jnp.concatenate([msgs[k][row0 : row0 + TILE, lane : lane + LEVEL] for k in range(UNIT)], axis=0)
            pieces.append(dot_nn(rows, order).astype(BF16))
        hot = jnp.concatenate(hots[a:], axis=1)
        out_vmem[a] = dot_nn(hot, jnp.concatenate(pieces, axis=0)).astype(BF16)
        copy = pltpu.make_async_copy(out_vmem.at[a], out.at[:, pl.ds(LEVEL * a, LEVEL)], sems.at[a])
        copy.start()
        copies.append(copy)
    for copy in copies:
        copy.wait()


def spec(space):
    return pl.BlockSpec(memory_space=space)


VM, SM, HB = pltpu.VMEM, pltpu.SMEM, pl.ANY


def call(kernel, args, spaces, outs, out_spaces, scratch, cost=None):
    return pl.pallas_call(
        kernel,
        out_shape=[jax.ShapeDtypeStruct(s, d) for s, d in outs],
        in_specs=[spec(s) for s in spaces],
        out_specs=[spec(s) for s in out_spaces],
        scratch_shapes=scratch,
        compiler_params=pltpu.CompilerParams(vmem_limit_bytes=VMEM_LIMIT),
        cost_estimate=cost,
    )(*args)


def solve_call(*args):
    return call(
        solve_kernel,
        args,
        (SM, SM) + (VM,) * 4,
        tuple(((2 * TILE, STATE_LANES), BF16) for _ in range(UNIT)) + (((UNIT, 2 * TILE, BS), BF16),),
        (VM,) * (UNIT + 1),
        [
            pltpu.VMEM((HALF_ROWS, COMPS * SLOTS, BS), F32),
            pltpu.VMEM((HALF_ROWS, COMPS * SLOTS, BS), BF16),
            pltpu.VMEM((HALF_ROWS, COMPS * SLOTS, BS), BF16),
            pltpu.VMEM((OFF_GRP, SLOTS, BS), F32),
            pltpu.VMEM((HALF_ROWS, SLOTS, BS), F32),
            pltpu.VMEM((NBMAX, SLOTS, BS), F32),
            pltpu.VMEM((HALF_ROWS // 2, 2 * BS, 2 * BS), BF16),
            pltpu.VMEM((OFF_GRP // 2, 2 * BS, 2 * BS), BF16),
        ],
    )


def pack_call(groups, rounds, *args):
    elems = args[1].shape[1]
    return call(
        functools.partial(pack_kernel, groups, rounds),
        args,
        (SM, VM, VM, VM, VM, HB),
        (((UNIT, 2 * TILE, MSG_LANES), BF16), ((8, elems), F32), ((8, elems), I32)),
        (VM,) * 3,
        [pltpu.VMEM((elems, NBMAX * LEVEL), BF16), pltpu.SemaphoreType.DMA],
    )


def unpack_call(*args):
    elems = args[1].shape[1]
    return call(
        unpack_kernel,
        args,
        (SM,) + (VM,) * (UNIT + 2),
        (((elems, NBMAX * LEVEL), BF16),),
        (HB,),
        [pltpu.VMEM((NBMAX, elems, LEVEL), BF16), pltpu.SemaphoreType.DMA((NBMAX,))],
    )


def on_device(
    shape,
    displacement, nodal_load, connectivity, shape_grads, elem_volume, point_map, vol_blocks, c_affine,
    coupling, diag_blocks, diag_normal, off_blocks, off_row, off_col, off_normal, off_count, fluct_state,
):
    z_count = shape[2]
    groups = z_count * 4
    rounds = z_count // 2
    devices = 4 * groups
    elems = connectivity.shape[1]
    node_count = displacement.shape[1]
    index = {name: lax.axis_index(name) for name in AXES}
    unit_index = index["x"] * 4 + index["l"] * 2 + index["c"]
    ids = jnp.stack(
        [index["y"], index["x"], index["h"], index["l"], index["c"], unit_index, unit_index, unit_index]
    ).astype(I32)

    def coords(device):
        section, group = divmod(device, groups)
        return section // 2, section % 2, group // 4, (group // 2) % 2, group % 2

    def number(y, x, h, l, c):
        return (y * 2 + x) * groups + h * 4 + l * 2 + c

    def permute(value, source_of):
        pairs = [(number(*source_of(*coords(d))), d) for d in range(devices)]
        return lax.ppermute(value, AXES, pairs)

    def unit_permute(value, k):
        return permute(value, lambda y, x, h, l, c: (y, x ^ (k >> 2), h, l ^ ((k >> 1) & 1), c ^ (k & 1)))

    def normal_rows(normals):
        return jnp.pad(normals.transpose(2, 1, 0)[:, 0], ((0, 2), (0, BS - normals.shape[0])))

    diag_half, small, ints = call(
        matrix_pack_kernel,
        (
            ids, vol_blocks, off_row.T, off_col.T, off_count, coupling.reshape(ROWS_GRP * COMPS, BS),
            normal_rows(diag_normal), normal_rows(off_normal), c_affine[0], diag_blocks[:, 0],
        ),
        (SM, SM, SM, SM, SM, VM, VM, VM, VM, HB),
        (((HALF_ROWS, BS, BS), BF16), ((SM_ROWS, BS), F32), ((8, BS), I32)),
        (VM, VM, SM),
        [
            pltpu.SMEM((32,), I32), pltpu.SMEM((32,), I32), pltpu.SMEM((16,), I32), pltpu.SMEM((8,), I32),
            pltpu.VMEM((ROWS_GRP * COMPS + 16, BS), F32),
            pltpu.SemaphoreType.DMA((HALF_ROWS,)),
        ],
    )
    packed, strain, place = pack_call(
        groups, rounds, ids, point_map.reshape(1, elems), displacement, connectivity, shape_grads, fluct_state
    )
    msgs = lax.all_to_all(packed, UNIT_AXES, split_axis=0, concat_axis=0, tiled=True)

    solved = None
    for turn in range(rounds):
        def from_group(y, x, h, l, c, turn=turn):
            return y, x, (h + 2 * turn + (x ^ c)) % z_count, l, c

        off_t, diag_t, small_t, ints_t = [
            permute(value, from_group) for value in (off_blocks[:, 0], diag_half, small, ints)
        ]
        (off_t,) = call(
            transpose_kernel,
            (off_t,),
            (VM,),
            (((OFF_GRP, BS, BS), BF16),),
            (VM,),
            [],
            pl.CostEstimate(flops=60_000_000_000, bytes_accessed=200_000_000, transcendentals=0),
        )
        result = solve_call(ids, ints_t, small_t, diag_t, off_t, msgs)
        if solved is None:
            solved = result
        else:
            of_turn = (jnp.arange(2 * TILE) % TILE) // (TILE // rounds) == turn
            solved = [jnp.where(of_turn[:, None], new, old) for new, old in zip(result, solved)]

    back = [solved[0]] + [unit_permute(solved[k], k) for k in range(1, UNIT)]
    own, back[4] = lax.optimization_barrier((solved[UNIT], back[4]))
    tangents = lax.all_to_all(own, UNIT_AXES, split_axis=0, concat_axis=0, tiled=True)
    residual, product, norm = call(
        fem_kernel,
        (ids, tangents, place, strain, shape_grads, elem_volume.reshape(1, elems), connectivity, nodal_load),
        (SM,) + (VM,) * 7,
        (((3, node_count), F32), ((3, node_count), F32), ((devices, BS), F32)),
        (VM,) * 3,
        [],
    )
    norms = lax.all_to_all(norm, AXES, split_axis=0, concat_axis=0, tiled=True)
    norm_sq = jnp.sum(norms[:, 0])
    root_mean = jnp.sqrt(norm_sq / (3.0 * node_count * devices) + 1e-06)
    update = -jnp.minimum(1.0, CLIP_RMS / root_mean) * residual
    (fluct_new,) = unpack_call(ids, place, tangents, *back)
    return residual, product, update, fluct_new


def solution(mesh):
    sections, groups = mesh.shape["sec"], mesh.shape["bulk"]
    shape = (2, sections // 2, groups // 4, 2, 2)
    fine = Mesh(mesh.devices.reshape(shape), AXES)
    return jax.shard_map(
        functools.partial(on_device, shape),
        mesh=fine,
        in_specs=(
            P(None, AXES),
            P(None, AXES),
            P(None, AXES),
            P(None, AXES),
            P(AXES),
            P(AXES),
            P(GROUP_AXES, None),
            P(GROUP_AXES, None, None),
            P(None, GROUP_AXES, None, None),
            P(None, GROUP_AXES, None, None),
            P(None, GROUP_AXES, None),
            P(None, GROUP_AXES, None, None),
            P(None, GROUP_AXES),
            P(None, GROUP_AXES),
            P(None, GROUP_AXES, None),
            P(GROUP_AXES),
            P(AXES, None),
        ),
        out_specs=(P(None, AXES), P(None, AXES), P(None, AXES), P(AXES, None)),
        check_vma=False,
    )
```

```python
import functools

import jax
import jax.numpy as jnp
from jax import lax
from jax.experimental import pallas as pl
from jax.experimental.pallas import tpu as pltpu
from jax.sharding import Mesh, PartitionSpec as P

BS = 128
NBMAX = 4
VOL_GRP = 8
GPV_DEV = 64
SWEEPS = 3
ROWS_GRP = 20
HALF_ROWS = 10
OFF_GRP = 32
HALF_OFF = 16
COMPS = 6
LEVEL = BS * COMPS
UNIT = 8
TILE = 16
SLOTS = UNIT * TILE
STATE_LANES = 5 * LEVEL
MSG_LANES = STATE_LANES + 128
GAIN_NORMAL = 0.4
WIDE = 8
CHUNK = 256
CLIP_RMS = 1.0
SM_NORMAL = 80
SM_AFFINE = 88
SM_ROWS = 96
RANK_LANE = 6

F32 = jnp.float32
BF16 = jnp.bfloat16
I32 = jnp.int32
AXES = ("y", "x", "h", "l", "c")
GROUP_AXES = ("h", "l", "c")
UNIT_AXES = ("x", "l", "c")
VMEM_LIMIT = 56 * 1024 * 1024

CLASS_PLACE = ((4 * LEVEL, 0), (3 * LEVEL, TILE), (0, TILE), (0, 0))
CLASS_BASE = (0, 1, 3, 6)


def dot_nn(lhs, rhs):
    return lax.dot_general(lhs, rhs, (((1,), (0,)), ((), ())), preferred_element_type=F32)


def dot_nt(lhs, rhs):
    return lax.dot_general(lhs, rhs, (((1,), (1,)), ((), ())), preferred_element_type=F32)


def dot_tn(lhs, rhs):
    return lax.dot_general(lhs, rhs, (((0,), (0,)), ((), ())), preferred_element_type=F32)


def split3(value):
    high = value.astype(BF16)
    rest = value - high.astype(F32)
    mid = rest.astype(BF16)
    low = (rest - mid.astype(F32)).astype(BF16)
    return high, mid, low


def iota(shape, dim):
    return lax.broadcasted_iota(I32, shape, dim)


def lane_order():
    target = iota((1, LEVEL), 1)
    source = COMPS * (target % BS) + target // BS
    return jnp.where(iota((LEVEL, LEVEL), 0) == source, 1.0, 0.0).astype(BF16)


def lane_order_back():
    row = iota((LEVEL, 1), 0)
    return jnp.where(iota((LEVEL, LEVEL), 1) == COMPS * (row % BS) + row // BS, 1.0, 0.0).astype(BF16)


def class_onehot(slot, size, level_rows):
    chosen = jnp.where(size == level_rows, slot, -1)
    return jnp.where(iota((SLOTS, slot.shape[1]), 0) == chosen, 1.0, 0.0).astype(BF16)


def returned_onehots(ids, tangents, slot, rank):
    packed, hots = [], [None] * NBMAX
    wanted = rank * SLOTS + slot
    place = iota((SLOTS, 1), 0)
    for row0, one, two in ((0, 3, 0), (TILE, 2, 1)):
        tile = jnp.concatenate([tangents[ids[5] ^ k, row0 : row0 + TILE, :] for k in range(UNIT)], axis=0)
        packed.append(tile)
        for c, lane in ((one, RANK_LANE), (two, 64 + RANK_LANE)):
            at = tile[:, lane : lane + 1].astype(F32).astype(I32) * SLOTS + place
            hots[c] = jnp.where(wanted == at, 1.0, 0.0).astype(BF16)
    return packed, hots


def node_onehot(conn_row, nodes):
    return jnp.where(iota((nodes, conn_row.shape[1]), 0) == conn_row, 1.0, 0.0).astype(BF16)


def nodal_parts(nodal):
    parts = [jnp.concatenate([p.astype(F32), jnp.zeros((13, p.shape[1]), F32)], axis=0) for p in split3(nodal)]
    rows = parts[0] + pltpu.roll(parts[1], 3, 0) + pltpu.roll(parts[2], 6, 0)
    return rows.astype(BF16)


def gather_nodes(rows, onehots):
    found = []
    for onehot in onehots:
        got = dot_nn(rows, onehot)
        found.append([got[i : i + 1] + got[i + 3 : i + 4] + got[i + 6 : i + 7] for i in range(3)])
    return found


def strain_rows(grads, disp):
    g = lambda a, k: grads[3 * a + k : 3 * a + k + 1]
    total = lambda f: f(0) + f(1) + f(2) + f(3)
    return [
        total(lambda a: g(a, 0) * disp[a][0]),
        total(lambda a: g(a, 1) * disp[a][1]),
        total(lambda a: g(a, 2) * disp[a][2]),
        total(lambda a: g(a, 2) * disp[a][1] + g(a, 1) * disp[a][2]),
        total(lambda a: g(a, 2) * disp[a][0] + g(a, 0) * disp[a][2]),
        total(lambda a: g(a, 1) * disp[a][0] + g(a, 0) * disp[a][1]),
    ]


def matrix_pack_kernel(
    ids, vol, off_row, off_col, off_count, coupling, diag_normal, off_normal, affine, diag,
    diag_out, small, ints, row_local, row_size, rows_sel, seen, loads, sems,
):
    half = ids[0]
    small[...] = jnp.zeros_like(small)
    loads[...] = jnp.zeros_like(loads)
    loads[0 : ROWS_GRP * COMPS, :] = coupling[...]
    small[0:VOL_GRP, 0:36] = affine[...]
    target = iota((1, BS), 1) % 64
    source = jnp.where(jnp.logical_and(target % 8 < 6, target < 48), 6 * (target % 8) + target // 8, -1)
    shift = jnp.where(iota((BS, BS), 0) == source, 1.0, 0.0).astype(BF16)
    moved = sum(dot_nn(part, shift) for part in split3(small[0:VOL_GRP, :]))
    small[0:VOL_GRP, :] = jnp.zeros((VOL_GRP, BS), F32)
    for size in range(NBMAX + 1):
        seen[size] = 0
    start = 0
    for v in range(VOL_GRP):
        size = vol[0, v]
        rank = seen[size]
        seen[size] = rank + 1
        mine = rank == half
        base = (size * (size - 1)) // 2
        for a in range(NBMAX):
            @pl.when(a < size)
            def _(a=a, size=size, base=base, mine=mine, start=start):
                row_local[start + a] = jnp.where(mine, base + a, -1)
                row_size[start + a] = size - 1

            @pl.when(jnp.logical_and(a < size, mine))
            def _(a=a, base=base, start=start):
                rows_sel[base + a] = start + a

        @pl.when(mine)
        def _(size=size, v=v):
            small[pl.ds(SM_AFFINE - 1 + size, 1), :] = moved[v : v + 1, :]
            ints[6, size - 1] = v

        start = start + size
    copies = []
    for i in range(HALF_ROWS):
        copies.append(
            pltpu.make_async_copy(diag.at[pl.ds(rows_sel[i], 1)], diag_out.at[pl.ds(i, 1)], sems.at[i])
        )
        copies[-1].start()
    lane = iota((8, BS), 1)
    normals = jnp.zeros((8, BS), F32)
    diag_rows = diag_normal[...]
    for i in range(HALF_ROWS):
        row = rows_sel[i]
        small[8 * i : 8 * i + COMPS, :] = loads[pl.ds(COMPS * row, COMPS), :]
        normals += jnp.where(lane == i, pltpu.roll(diag_rows, (i - row + BS) % BS, 1), 0.0)
    normals += pltpu.roll(off_normal[...], HALF_OFF, 1)
    small[SM_NORMAL : SM_NORMAL + 8, :] = normals
    live_total = off_count[0]

    def contact(n, found):
        row = off_row[0, n]
        local = row_local[row]
        ints[4, n] = jnp.maximum(local, 0)
        ints[5, n] = row_size[row]
        live = jnp.logical_and(n < live_total, local >= 0)

        @pl.when(live)
        def _():
            ints[1, found] = n
            ints[2, found] = local
            ints[3, found] = row_local[off_col[0, n]]

        return found + live.astype(I32)

    ints[0, 0] = lax.fori_loop(0, OFF_GRP, contact, 0)
    for copy in copies:
        copy.wait()


def pack_kernel(groups, rounds, ids, point_map, disp, conn, grads, state, *refs):
    out, strain_out, place_out, state_vmem, sem = refs
    load = pltpu.make_async_copy(state, state_vmem, sem)
    load.start()
    elems = point_map.shape[1]
    x_me, h_me, l_me, c_me = ids[1], ids[2], ids[3], ids[4]
    z_count = groups // 4
    codes = point_map[...]
    owner = codes // elems
    within = codes % elems
    group = owner % groups
    volume = within // GPV_DEV
    delta = (group // 4 - h_me + z_count) % z_count
    core = group % 2
    low = (group // 2) % 2
    across = (delta % 2) ^ core
    turn = delta // 2
    offset = ((across ^ x_me) * 4) + ((low ^ l_me) * 2) + (core ^ c_me)
    volumes = groups * VOL_GRP
    volume_hot = iota((volumes, elems), 0) == group * VOL_GRP + volume
    volume_hot16 = jnp.where(volume_hot, 1.0, 0.0).astype(BF16)
    load.wait()
    level_lane = iota((1, BS), 1)
    filled = jnp.where(level_lane == NBMAX, 1.0, 0.0)
    for a in range(NBMAX):
        chosen = jnp.where(iota((LEVEL, BS), 1) == a, 1.0, 0.0).astype(BF16)
        filled = filled + dot_nn(jnp.abs(state_vmem[:, LEVEL * a : LEVEL * (a + 1)]), chosen)
    marks = dot_nn(volume_hot16, jnp.where(filled > 0.0, 1.0, 0.0).astype(BF16))

    def code_of(take, counts, number):
        height = jnp.zeros_like(number)
        for a in range(NBMAX):
            height = jnp.where(take(counts, a) > 0.0, a + 1, height)
        return jnp.where(take(counts, NBMAX) > 0.0, height * VOL_GRP + number % VOL_GRP, 1 << 20)

    code_row = code_of(
        lambda x, a: x[a : a + 1, :], jnp.transpose(marks), iota((1, volumes), 1)
    )
    code_col = code_of(
        lambda x, a: x[:, a : a + 1], marks, iota((volumes, 1), 0)
    )
    same = iota((volumes, volumes), 0) // VOL_GRP == iota((volumes, volumes), 1) // VOL_GRP
    below = jnp.where(jnp.logical_and(same, code_row < code_col), 1, 0)
    rank_col = jnp.sum(below, axis=1, keepdims=True) + 1
    size = jnp.sum(jnp.where(volume_hot, rank_col, 0), axis=0, keepdims=True)
    key = (offset * NBMAX + size - 1) * rounds + turn
    key_hot = iota((UNIT * NBMAX * rounds, elems), 0) == key
    earlier = jnp.where(iota((elems, elems), 0) < iota((elems, elems), 1), 1.0, 0.0).astype(BF16)
    counts = dot_nn(jnp.where(key_hot, 1.0, 0.0).astype(BF16), earlier)
    rank = jnp.sum(jnp.where(key_hot, counts, 0.0), axis=0, keepdims=True).astype(I32)
    slot = offset * TILE + turn * (TILE // rounds) + rank
    place_out[...] = jnp.concatenate([slot, size, jnp.zeros((6, elems), I32)], axis=0)

    nodes = disp.shape[1]
    onehots = [node_onehot(conn[a : a + 1, :], nodes) for a in range(4)]
    found = gather_nodes(nodal_parts(disp[...]), onehots)
    strain = strain_rows(grads[...], found)
    strain8 = jnp.concatenate(strain + [volume.astype(F32), jnp.zeros((1, elems), F32)], axis=0)
    strain_out[...] = strain8
    first = jnp.concatenate([strain8, jnp.zeros((120, elems), F32)], axis=0).astype(BF16)
    second = jnp.concatenate(
        [jnp.zeros((64, elems), F32), strain8, jnp.zeros((56, elems), F32)], axis=0
    ).astype(BF16)
    hots = [class_onehot(slot, size, c + 1) for c in range(NBMAX)]
    for one, other, row0 in ((3, 0, 0), (2, 1, TILE)):
        extras = (dot_nt(hots[one], first) + dot_nt(hots[other], second)).astype(BF16)
        for k in range(UNIT):
            out[ids[5] ^ k, row0 : row0 + TILE, STATE_LANES:] = extras[TILE * k : TILE * (k + 1)]
    order = lane_order()
    for c in range(NBMAX):
        lane0, row0 = CLASS_PLACE[c]
        for a in range(c + 1):
            rows = dot_nn(hots[c], state_vmem[:, LEVEL * a : LEVEL * (a + 1)]).astype(BF16)
            rows = dot_nn(rows, order).astype(BF16)
            for k in range(UNIT):
                out[ids[5] ^ k, row0 : row0 + TILE, lane0 + LEVEL * a : lane0 + LEVEL * (a + 1)] = rows[
                    TILE * k : TILE * (k + 1)
                ]


def transpose_kernel(off, turned):
    for n in range(OFF_GRP):
        turned[n] = jnp.transpose(off[n])


def solve_kernel(ids, ints, small, blocks, off, msgs, *refs):
    outs, refs = refs[:UNIT], refs[UNIT:]
    tangents, state, low, rest, contact_scale, inverse, response, diag_pairs, off_pairs = refs
    extras = []
    for rank in range(NBMAX):
        row0 = CLASS_PLACE[rank][1]
        tile = jnp.concatenate([msgs[ids[5] ^ k, row0 : row0 + TILE, STATE_LANES:] for k in range(UNIT)], axis=0).astype(F32)
        extras.append(tile if rank >= 2 else pltpu.roll(tile, 64, 1))
    held = [[extras[rank][:, RANK_LANE : RANK_LANE + 1] == ints[6, c].astype(F32) for rank in range(NBMAX)] for c in range(NBMAX)]
    agree = functools.reduce(jnp.logical_and, [held[c][c] for c in range(NBMAX)])
    in_order = jnp.min(jnp.where(agree, 1.0, 0.0)) > 0.5

    @pl.when(in_order)
    def _():
        for c in range(NBMAX):
            lane0, row0 = CLASS_PLACE[c]
            for a in range(c + 1):
                r = CLASS_BASE[c] + a
                for j in range(COMPS):
                    lane = lane0 + LEVEL * a + BS * j
                    for k in range(UNIT):
                        piece = msgs[ids[5] ^ k, row0 : row0 + TILE, lane : lane + BS]
                        dst = slice(SLOTS * j + TILE * k, SLOTS * j + TILE * (k + 1))
                        low[r, dst, :] = piece
                        state[r, dst, :] = piece.astype(F32)

    @pl.when(jnp.logical_not(in_order))
    def _():
        def component(j, carry):
            for c in range(NBMAX):
                for a in range(c + 1):
                    r = CLASS_BASE[c] + a
                    total = jnp.zeros((SLOTS, BS), F32)
                    for rank in range(a, NBMAX):
                        lane0, row0 = CLASS_PLACE[rank]
                        lane = pl.multiple_of(lane0 + LEVEL * a + BS * j, BS)
                        piece = jnp.concatenate(
                            [msgs[ids[5] ^ k, row0 : row0 + TILE, pl.ds(lane, BS)] for k in range(UNIT)], axis=0
                        )
                        total = jnp.where(held[c][rank], piece.astype(F32), total)
                    dst = pl.ds(pl.multiple_of(SLOTS * j, SLOTS), SLOTS)
                    low[r, dst, :] = total.astype(BF16)
                    state[r, dst, :] = total
            return carry

        lax.fori_loop(0, COMPS, component, 0)

    normals = small[SM_NORMAL : SM_NORMAL + 8, :]
    normals = jnp.concatenate([normals, jnp.zeros((BS - 8, BS), F32)], axis=0)
    parts = split3(normals)
    for c in range(NBMAX):
        strains = jnp.zeros((SLOTS, BS), F32)
        for rank in range(NBMAX):
            strains = jnp.where(held[c][rank], extras[rank], strains)
        strains = strains.astype(BF16)
        dots = dot_nn(strains, parts[0]) + dot_nn(strains, parts[1]) + dot_nn(strains, parts[2])
        response[c] = 1.0 + GAIN_NORMAL * jnp.tanh(dots)
    eye = iota((BS, BS), 0) == iota((BS, BS), 1)
    diag_inverse = []
    for c in range(NBMAX):
        for a in range(c + 1):
            r = CLASS_BASE[c] + a
            values = jnp.sum(jnp.where(eye, blocks[r].astype(F32), 0.0), axis=0, keepdims=True)
            diag_inverse.append(1.0 / values)
            inverse[r] = jnp.broadcast_to(1.0 / response[c, :, r : r + 1], (SLOTS, BS)) * diag_inverse[r]
    for n in range(OFF_GRP):
        contact_scale[n] = (
            jnp.broadcast_to(response[ints[5, n], :, HALF_OFF + n : HALF_OFF + n + 1], (SLOTS, BS))
            * inverse[ints[4, n]]
        )
    zero = jnp.zeros((BS, BS), BF16)
    for p in range(HALF_ROWS // 2):
        diag_pairs[p, :BS, :BS] = blocks[2 * p]
        diag_pairs[p, :BS, BS:] = zero
        diag_pairs[p, BS:, :BS] = zero
        diag_pairs[p, BS:, BS:] = blocks[2 * p + 1]
    live = ints[0, 0]
    turns = (live + WIDE - 1) // WIDE

    def contact_block(m):
        n = ints[1, jnp.minimum(m, live - 1)]
        found = off[n]
        return jnp.where(m < live, found, zero)

    def fill(p, carry):
        off_pairs[p, :BS, :BS] = contact_block(2 * p)
        off_pairs[p, :BS, BS:] = zero
        off_pairs[p, BS:, :BS] = zero
        off_pairs[p, BS:, BS:] = contact_block(2 * p + 1)
        return carry

    lax.fori_loop(0, turns * (WIDE // 2), fill, 0)

    def contacts(t, carry):
        slots = [jnp.minimum(WIDE * t + i, live - 1) for i in range(WIDE)]
        cols = [ints[3, m] for m in slots]
        rows = [ints[2, m] for m in slots]
        which = [ints[1, m] for m in slots]
        for base in range(0, COMPS * SLOTS, CHUNK):
            span = slice(base, base + CHUNK)
            products = []
            for h in range(WIDE // 2):
                both = jnp.concatenate([low[cols[2 * h], span, :], low[cols[2 * h + 1], span, :]], axis=1)
                products.append(dot_nn(both, off_pairs[(WIDE // 2) * t + h]))
            for i in range(WIDE):
                scale = contact_scale[which[i]]
                for j in range(CHUNK // SLOTS):
                    part = products[i // 2][SLOTS * j : SLOTS * (j + 1), BS * (i % 2) : BS * (i % 2 + 1)]
                    state[rows[i], base + SLOTS * j : base + SLOTS * (j + 1), :] -= part * scale
        return carry

    def sweep(last):
        lax.fori_loop(0, turns, contacts, 0)
        for p in range(HALF_ROWS // 2):
            for base in range(0, COMPS * SLOTS, CHUNK):
                span = slice(base, base + CHUNK)
                both = jnp.concatenate([low[2 * p, span, :], low[2 * p + 1, span, :]], axis=1)
                product = dot_nt(both, diag_pairs[p])
                for i in range(2):
                    r = 2 * p + i
                    for j in range(CHUNK // SLOTS):
                        comp = base // SLOTS + j
                        at = slice(SLOTS * comp, SLOTS * (comp + 1))
                        part = product[SLOTS * j : SLOTS * (j + 1), BS * i : BS * (i + 1)]
                        load = small[8 * r + comp : 8 * r + comp + 1, :]
                        value = state[r, at, :] + (load * inverse[r] - part * diag_inverse[r])
                        high = value.astype(BF16)
                        low[r, at, :] = high
                        if last:
                            rest[r, at, :] = (value - high.astype(F32)).astype(BF16)
                        else:
                            state[r, at, :] = value

    lax.fori_loop(0, SWEEPS - 1, lambda step, carry: (sweep(False), carry)[1], 0)
    sweep(True)
    lane = iota((1, BS), 1)
    entries = []
    for c in range(NBMAX):
        weights, values = [], []
        for a in range(c + 1):
            r = CLASS_BASE[c] + a
            load8 = small[8 * r : 8 * r + 8, :]
            high = load8.astype(BF16).astype(F32)
            gap = jnp.zeros((16, BS), F32)
            both = jnp.concatenate([high] * 6 + [gap] + [load8 - high] * 6 + [gap], axis=0).astype(BF16)
            weights += [both, both]
            values += [low[r], rest[r]]
        product = dot_nt(jnp.concatenate(values, axis=1), jnp.concatenate(weights, axis=1))
        total = jnp.zeros((SLOTS, BS), F32)
        for j in range(COMPS):
            total = jnp.where((lane // 8) % 8 == j, product[SLOTS * j : SLOTS * (j + 1)], total)
        total = total + pltpu.roll(total, 64, 1)
        found = sum(jnp.where(held[c][rank], rank + 1.0, 0.0) for rank in range(NBMAX))
        entry = small[SM_AFFINE + c : SM_AFFINE + c + 1, :] - total / ((c + 1) * BS)
        entries.append(jnp.where(lane % 64 == RANK_LANE, found, entry))
    for row0, one, two in ((0, 3, 0), (TILE, 2, 1)):
        packed = jnp.where(lane < 64, entries[one], entries[two]).astype(BF16)
        for k in range(UNIT):
            tangents[ids[5] ^ k, row0 : row0 + TILE, :] = packed[TILE * k : TILE * (k + 1)]
    for c in range(NBMAX):
        lane0, row0 = CLASS_PLACE[c]
        for a in range(c + 1):
            r = CLASS_BASE[c] + a
            for j in range(COMPS):
                lane_at = lane0 + LEVEL * a + BS * j
                for k in range(UNIT):
                    outs[k][row0 : row0 + TILE, lane_at : lane_at + BS] = low[
                        r, SLOTS * j + TILE * k : SLOTS * j + TILE * (k + 1), :
                    ]


def fem_kernel(ids, tangents, place, strain, grads, volume, conn, nodal_load, residual, product, norm):
    elems = place.shape[1]
    nodes = nodal_load.shape[1]
    slot, size = place[0:1, :], place[1:2, :]
    packed, hots = returned_onehots(ids, tangents, slot, size)
    entries = jnp.zeros((64, elems), F32)
    for tile, one, two in ((packed[0], 3, 0), (packed[1], 2, 1)):
        entries += dot_tn(tile, hots[one])[:64]
        entries += dot_tn(tile, hots[two])[64:]
    entry = lambda i, j: entries[8 * j + i : 8 * j + i + 1]
    weight = volume[...]
    g_all = grads[...]
    g = lambda a, k: g_all[3 * a + k : 3 * a + k + 1]
    onehots = [node_onehot(conn[a : a + 1, :], nodes) for a in range(4)]

    def assemble(strains):
        s = []
        for i in range(COMPS):
            total = entry(i, 0) * strains[0]
            for j in range(1, COMPS):
                total = total + entry(i, j) * strains[j]
            s.append(total * weight)
        result = jnp.zeros((TILE, nodes), F32)
        for a in range(4):
            force = jnp.concatenate(
                [
                    g(a, 0) * s[0] + g(a, 2) * s[4] + g(a, 1) * s[5],
                    g(a, 1) * s[1] + g(a, 2) * s[3] + g(a, 0) * s[5],
                    g(a, 2) * s[2] + g(a, 1) * s[3] + g(a, 0) * s[4],
                ],
                axis=0,
            )
            result += dot_nt(nodal_parts(force), onehots[a])
        return result[0:3] + result[3:6] + result[6:9]

    strains = strain[...]
    res = assemble([strains[i : i + 1] for i in range(COMPS)]) - nodal_load[...]
    residual[...] = res
    norm[...] = jnp.broadcast_to(jnp.sum(res * res, keepdims=True), norm.shape)
    trial = strain_rows(g_all, gather_nodes(nodal_parts(res), onehots))
    product[...] = assemble(trial)


def unpack_kernel(ids, place, tangents, *refs):
    msgs, (out, out_vmem, sems) = refs[:UNIT], refs[UNIT:]
    slot, size = place[0:1, :], place[1:2, :]
    order = lane_order_back()
    hots = [jnp.transpose(hot) for hot in returned_onehots(ids, tangents, slot, size)[1]]
    copies = []
    for a in range(NBMAX):
        pieces = []
        for c in range(a, NBMAX):
            lane0, row0 = CLASS_PLACE[c]
            lane = lane0 + LEVEL * a
            rows = jnp.concatenate([msgs[k][row0 : row0 + TILE, lane : lane + LEVEL] for k in range(UNIT)], axis=0)
            pieces.append(dot_nn(rows, order).astype(BF16))
        hot = jnp.concatenate(hots[a:], axis=1)
        out_vmem[a] = dot_nn(hot, jnp.concatenate(pieces, axis=0)).astype(BF16)
        copy = pltpu.make_async_copy(out_vmem.at[a], out.at[:, pl.ds(LEVEL * a, LEVEL)], sems.at[a])
        copy.start()
        copies.append(copy)
    for copy in copies:
        copy.wait()


def spec(space):
    return pl.BlockSpec(memory_space=space)


VM, SM, HB = pltpu.VMEM, pltpu.SMEM, pl.ANY


def call(kernel, args, spaces, outs, out_spaces, scratch, cost=None):
    return pl.pallas_call(
        kernel,
        out_shape=[jax.ShapeDtypeStruct(s, d) for s, d in outs],
        in_specs=[spec(s) for s in spaces],
        out_specs=[spec(s) for s in out_spaces],
        scratch_shapes=scratch,
        compiler_params=pltpu.CompilerParams(vmem_limit_bytes=VMEM_LIMIT),
        cost_estimate=cost,
    )(*args)


def solve_call(*args):
    return call(
        solve_kernel,
        args,
        (SM, SM) + (VM,) * 4,
        tuple(((2 * TILE, STATE_LANES), BF16) for _ in range(UNIT)) + (((UNIT, 2 * TILE, BS), BF16),),
        (VM,) * (UNIT + 1),
        [
            pltpu.VMEM((HALF_ROWS, COMPS * SLOTS, BS), F32),
            pltpu.VMEM((HALF_ROWS, COMPS * SLOTS, BS), BF16),
            pltpu.VMEM((HALF_ROWS, COMPS * SLOTS, BS), BF16),
            pltpu.VMEM((OFF_GRP, SLOTS, BS), F32),
            pltpu.VMEM((HALF_ROWS, SLOTS, BS), F32),
            pltpu.VMEM((NBMAX, SLOTS, BS), F32),
            pltpu.VMEM((HALF_ROWS // 2, 2 * BS, 2 * BS), BF16),
            pltpu.VMEM((OFF_GRP // 2, 2 * BS, 2 * BS), BF16),
        ],
    )


def pack_call(groups, rounds, *args):
    elems = args[1].shape[1]
    return call(
        functools.partial(pack_kernel, groups, rounds),
        args,
        (SM, VM, VM, VM, VM, HB),
        (((UNIT, 2 * TILE, MSG_LANES), BF16), ((8, elems), F32), ((8, elems), I32)),
        (VM,) * 3,
        [pltpu.VMEM((elems, NBMAX * LEVEL), BF16), pltpu.SemaphoreType.DMA],
    )


def unpack_call(*args):
    elems = args[1].shape[1]
    return call(
        unpack_kernel,
        args,
        (SM,) + (VM,) * (UNIT + 2),
        (((elems, NBMAX * LEVEL), BF16),),
        (HB,),
        [pltpu.VMEM((NBMAX, elems, LEVEL), BF16), pltpu.SemaphoreType.DMA((NBMAX,))],
    )


def on_device(
    shape,
    displacement, nodal_load, connectivity, shape_grads, elem_volume, point_map, vol_blocks, c_affine,
    coupling, diag_blocks, diag_normal, off_blocks, off_row, off_col, off_normal, off_count, fluct_state,
):
    z_count = shape[2]
    groups = z_count * 4
    rounds = z_count // 2
    devices = 4 * groups
    elems = connectivity.shape[1]
    node_count = displacement.shape[1]
    index = {name: lax.axis_index(name) for name in AXES}
    unit_index = index["x"] * 4 + index["l"] * 2 + index["c"]
    ids = jnp.stack(
        [index["y"], index["x"], index["h"], index["l"], index["c"], unit_index, unit_index, unit_index]
    ).astype(I32)

    def coords(device):
        section, group = divmod(device, groups)
        return section // 2, section % 2, group // 4, (group // 2) % 2, group % 2

    def number(y, x, h, l, c):
        return (y * 2 + x) * groups + h * 4 + l * 2 + c

    def permute(value, source_of):
        pairs = [(number(*source_of(*coords(d))), d) for d in range(devices)]
        return lax.ppermute(value, AXES, pairs)

    def unit_permute(value, k):
        return permute(value, lambda y, x, h, l, c: (y, x ^ (k >> 2), h, l ^ ((k >> 1) & 1), c ^ (k & 1)))

    def normal_rows(normals):
        return jnp.pad(normals.transpose(2, 1, 0)[:, 0], ((0, 2), (0, BS - normals.shape[0])))

    diag_half, small, ints = call(
        matrix_pack_kernel,
        (
            ids, vol_blocks, off_row.T, off_col.T, off_count, coupling.reshape(ROWS_GRP * COMPS, BS),
            normal_rows(diag_normal), normal_rows(off_normal), c_affine[0], diag_blocks[:, 0],
        ),
        (SM, SM, SM, SM, SM, VM, VM, VM, VM, HB),
        (((HALF_ROWS, BS, BS), BF16), ((SM_ROWS, BS), F32), ((8, BS), I32)),
        (VM, VM, SM),
        [
            pltpu.SMEM((32,), I32), pltpu.SMEM((32,), I32), pltpu.SMEM((16,), I32), pltpu.SMEM((8,), I32),
            pltpu.VMEM((ROWS_GRP * COMPS + 16, BS), F32),
            pltpu.SemaphoreType.DMA((HALF_ROWS,)),
        ],
    )
    packed, strain, place = pack_call(
        groups, rounds, ids, point_map.reshape(1, elems), displacement, connectivity, shape_grads, fluct_state
    )
    msgs = lax.all_to_all(packed, UNIT_AXES, split_axis=0, concat_axis=0, tiled=True)

    solved = None
    for turn in range(rounds):
        def from_group(y, x, h, l, c, turn=turn):
            return y, x, (h + 2 * turn + (x ^ c)) % z_count, l, c

        off_t, diag_t, small_t, ints_t = [
            permute(value, from_group) for value in (off_blocks[:, 0], diag_half, small, ints)
        ]
        (off_t,) = call(
            transpose_kernel,
            (off_t,),
            (VM,),
            (((OFF_GRP, BS, BS), BF16),),
            (VM,),
            [],
            pl.CostEstimate(flops=60_000_000_000, bytes_accessed=200_000_000, transcendentals=0),
        )
        result = solve_call(ids, ints_t, small_t, diag_t, off_t, msgs)
        if solved is None:
            solved = result
        else:
            of_turn = (jnp.arange(2 * TILE) % TILE) // (TILE // rounds) == turn
            solved = [jnp.where(of_turn[:, None], new, old) for new, old in zip(result, solved)]

    back = [solved[0]] + [unit_permute(solved[k], k) for k in range(1, UNIT)]
    own, back[4] = lax.optimization_barrier((solved[UNIT], back[4]))
    tangents = lax.all_to_all(own, UNIT_AXES, split_axis=0, concat_axis=0, tiled=True)
    residual, product, norm = call(
        fem_kernel,
        (ids, tangents, place, strain, shape_grads, elem_volume.reshape(1, elems), connectivity, nodal_load),
        (SM,) + (VM,) * 7,
        (((3, node_count), F32), ((3, node_count), F32), ((devices, BS), F32)),
        (VM,) * 3,
        [],
    )
    norms = lax.all_to_all(norm, AXES, split_axis=0, concat_axis=0, tiled=True)
    norm_sq = jnp.sum(norms[:, 0])
    root_mean = jnp.sqrt(norm_sq / (3.0 * node_count * devices) + 1e-06)
    update = -jnp.minimum(1.0, CLIP_RMS / root_mean) * residual
    (fluct_new,) = unpack_call(ids, place, tangents, *back)
    return residual, product, update, fluct_new


def solution(mesh):
    sections, groups = mesh.shape["sec"], mesh.shape["bulk"]
    shape = (2, sections // 2, groups // 4, 2, 2)
    fine = Mesh(mesh.devices.reshape(shape), AXES)
    return jax.shard_map(
        functools.partial(on_device, shape),
        mesh=fine,
        in_specs=(
            P(None, AXES),
            P(None, AXES),
            P(None, AXES),
            P(None, AXES),
            P(AXES),
            P(AXES),
            P(GROUP_AXES, None),
            P(GROUP_AXES, None, None),
            P(None, GROUP_AXES, None, None),
            P(None, GROUP_AXES, None, None),
            P(None, GROUP_AXES, None),
            P(None, GROUP_AXES, None, None),
            P(None, GROUP_AXES),
            P(None, GROUP_AXES),
            P(None, GROUP_AXES, None),
            P(GROUP_AXES),
            P(AXES, None),
        ),
        out_specs=(P(None, AXES), P(None, AXES), P(None, AXES), P(AXES, None)),
        check_vma=False,
    )
```
